256 devices in a mesh: section: 16 (over x_hi, z), fsdp: 16 (over x_lo, y, core).
Axes of the slice: x: 4 (x_hi: 2, x_lo: 2; x = x_hi * 2 + x_lo), y: 4, z: 8, core: 2. Of those that a mesh axis runs over, the one named last changes fastest.
Arguments:
- acts: bfloat16 [16, 9216, 2048], P('section', 'fsdp'), may hold values from -6 to 6
- gains: float32 [16, 2048], P('section'), may hold values from 0.5 to 1.5
- proj: bfloat16 [16, 2048, 2048], P('section', 'fsdp'), may hold values from -0.0625 to 0.0625
- head: bfloat16 [2048, 512], replicated, may hold values from -1 to 1
- segs: int32 [48, 192], P('fsdp'), may hold values from 0 to 15, never falling along the last dimension, each value on 1 to 24 neighbouring positions
- labels: int32 [48, 16], P('fsdp'), may hold values from 0 to 511
Outputs:
- din: bfloat16 [16, 9216, 2048], P('section', 'fsdp')
- dproj: bfloat16 [16, 2048, 2048], P('section', 'fsdp')
- dgain: float32 [16, 2048], P('section')
The draws below stay inside these ranges and needn't reach their ends.
Inputs may be any that keep to these rules, and one draw needn't show every extreme that they name: `segs`: each row lists the candidates of one microbatch in order, every candidate has at least one token and one has 24.
All inputs are finite; a program needn't handle non-finite values.
Results may differ from the reference program's by a relative error of at most 0.04.
Values may be sent and summed in bfloat16 or wider, within the bound.
No kernel may reach another device: no remote copies, remote signals or barrier semaphores. Data moves between devices by JAX's collectives and lax.ppermute only.
A program may use at most 128 MiB of HBM per device.

```python
import math
import jax
import jax.numpy as jnp
import numpy as np
from jax import lax

D = 2048
NCLS = 512
ROWS = 192
MOST = 24
CAND = 16
MBALL = 48
TOKENS = 9216
SECTIONS = 16


def touch_ends(result, own_key, least, high):
    longest = result.shape.index(max(result.shape))
    spots = []
    for shift in (0, 1):
        where = [jax.random.randint(jax.random.fold_in(own_key, axis), (), 0, length) for axis, length in enumerate(result.shape)]
        where[longest] = (where[longest] + shift) % result.shape[longest]
        spots.append(tuple(where))
    return result.at[spots[0]].set(least).at[spots[1]].set(high)


def shard_levels(rng, dims, shards, least, high):
    loudness = 1.0
    for position, shards_of in shards:
        steps = jax.random.uniform(jax.random.fold_in(jax.random.fold_in(rng, 6), position), (shards_of,), jnp.float32, least / len(shards), high / len(shards))
        loudness = loudness * jnp.repeat(jnp.exp(steps), dims[position] // shards_of).reshape((-1,) + (1,) * (len(dims) - 1 - position))
    return loudness


def profile(amount, total, reach, skew):
    weights = [(1 << 20) // math.isqrt(rank ** skew) + 1 for rank in range(2, amount + 1)]
    rest, given = total - reach - (amount - 1), [1] * (amount - 1)
    while rest > 0:
        movable = [i for i in range(amount - 1) if given[i] < reach]
        mass, remaining = sum([weights[i] for i in movable]), rest
        for i in movable:
            addition = min(reach - given[i], max(1, remaining * weights[i] // mass), rest)
            given[i] = given[i] + addition
            rest = rest - addition
    return np.array([reach] + given)


def uneven(rng, amount, total, limit, skew):
    if amount == 2:
        one = jax.random.randint(rng, (), max(1, total - limit), min(limit, total - 1) + 1)
        return jnp.stack([one, total - one])
    sizes = jnp.asarray(profile(amount, total, limit, skew), jnp.int32)
    pairs = (amount - 1) // 2
    source_of, sink = sizes[1:1 + 2 * pairs:2], sizes[2:2 + 2 * pairs:2]
    room = jnp.minimum(source_of - 1, limit - sink)
    shifted = jax.random.randint(jax.random.fold_in(rng, 1), (pairs,), 0, 1 << 20) % (room + 1)
    sizes = sizes.at[1:1 + 2 * pairs:2].set(source_of - shifted).at[2:2 + 2 * pairs:2].set(sink + shifted)
    return sizes[jax.random.permutation(jax.random.fold_in(rng, 2), amount)]


def scatter_about(rng, extent, scale, limit, shards=(), held_as=jnp.bfloat16):
    entries = scale * jax.random.normal(rng, extent, jnp.float32)
    if shards:
        entries = entries * shard_levels(rng, extent, shards, -0.22, 0.18)
    return jnp.clip(entries, -limit, limit).astype(held_as)


def setup_inputs(seed: int = 0) -> dict:
    arg_keys = jax.random.split(jax.random.key(seed), 7)
    acts = scatter_about(arg_keys[0], (SECTIONS, TOKENS, D), 1.0, 6.0, ((0, 16), (1, 16)))
    gains = jnp.clip(1.0 + 0.1 * jax.random.normal(arg_keys[1], (SECTIONS, D), jnp.float32), 0.5, 1.5)
    proj = scatter_about(arg_keys[2], (SECTIONS, D, D), (4 * D) ** -0.5, 0.0625, ((0, 16), (1, 16)))
    head = scatter_about(arg_keys[3], (D, NCLS), (D // 64) ** -0.5, 1.0)
    segs = jax.vmap(lambda own: jnp.searchsorted(jnp.cumsum(uneven(own, CAND, ROWS, MOST, 1)), jnp.arange(ROWS), side="right"))(jax.random.split(arg_keys[4], MBALL)).reshape((MBALL, ROWS)).astype(jnp.int32)
    labels = touch_ends(jax.random.randint(arg_keys[5], (MBALL, CAND), 0, NCLS), jax.random.fold_in(arg_keys[5], 1), 0, NCLS - 1).astype(jnp.int32)
    return {"acts": acts, "gains": gains, "proj": proj, "head": head, "segs": segs, "labels": labels}


norm_eps = 1e-06

def section_norm(layer_in, gain):
    x_float = layer_in.astype(jnp.float32)
    inv_rms = lax.rsqrt(lax.optimization_barrier(jnp.mean(x_float * x_float, -1, keepdims=True)) + norm_eps)
    x_hat = x_float * inv_rms
    return (x_hat, inv_rms, (x_hat * gain).astype(jnp.bfloat16))

def reference(acts, gains, proj, head, segs, labels):
    top = SECTIONS - 1
    x_hat, inv_rms, normed = section_norm(acts[top], gains[top])
    y_top = acts[top].astype(jnp.float32) + jnp.dot(normed, proj[top], preferred_element_type=jnp.float32)
    y_blocks = y_top.reshape(MBALL, ROWS, D)
    onehot = (segs[:, None, :] == jnp.arange(CAND, dtype=jnp.int32)[None, :, None]).astype(jnp.float32)
    counts = lax.optimization_barrier(jnp.sum(onehot, -1))
    pooled = (jnp.einsum('mcr,mrd->mcd', onehot, y_blocks) / counts[..., None]).astype(jnp.bfloat16)
    logits = jnp.dot(pooled.reshape(-1, D), head, preferred_element_type=jnp.float32)
    target = (labels.reshape(-1)[:, None] == jnp.arange(NCLS, dtype=jnp.int32)[None, :]).astype(jnp.float32)
    dlogit = (jax.nn.sigmoid(logits) - target).astype(jnp.bfloat16)
    dpool = jnp.dot(dlogit, head.T, preferred_element_type=jnp.float32).reshape(MBALL, CAND, D) / counts[..., None]
    grad = jnp.einsum('mcr,mcd->mrd', onehot, dpool).reshape(TOKENS, D).astype(jnp.bfloat16)
    din_list, dproj_list, dgain_list = ([], [], [])
    for section in reversed(range(SECTIONS)):
        x_hat, inv_rms, normed = section_norm(acts[section], gains[section])
        back = lax.dot_general(grad, proj[section], (((1,), (1,)), ((), ())), preferred_element_type=jnp.float32)
        scaled = back * gains[section]
        through = inv_rms * (scaled - x_hat * lax.optimization_barrier(jnp.mean(scaled * x_hat, -1, keepdims=True)))
        layer_grad = (grad.astype(jnp.float32) + through).astype(jnp.bfloat16)
        dgain_list.append(lax.optimization_barrier(jnp.sum(back * x_hat, 0)))
        weight_grad = lax.dot_general(normed, grad, (((0,), (0,)), ((), ())), preferred_element_type=jnp.float32)
        dproj_list.append(weight_grad.astype(jnp.bfloat16))
        din_list.append(layer_grad)
        grad = layer_grad
    din = jnp.stack(din_list[::-1])
    dproj = jnp.stack(dproj_list[::-1])
    dgain = jnp.stack(dgain_list[::-1])
    return (din, dproj, dgain)
```

```python
import functools

import jax
import jax.numpy as jnp
from jax import lax
from jax.experimental import pallas as pl
from jax.experimental.pallas import tpu as pltpu
from jax.sharding import PartitionSpec as P

norm_eps = 1e-06
piece = 48
lag = 2


def step_kernel(
    step,
    last,
    place,
    recv,
    weight,
    acts,
    rms,
    gain,
    grads_in,
    din_in,
    acc_in,
    out,
    grads,
    din,
    acc,
):
    rows, width = recv.shape
    index = step - lag * place[0]

    @pl.when((index >= 0) & (index <= last))
    def _():
        row = pl.multiple_of(index * rows, 16)
        here = pl.ds(row, rows)

        @pl.when(place[0] > 0)
        def _():
            grads[here, :] = recv[...]

        grad = grads[here, :]
        back = lax.dot_general(
            grad, weight[...], (((1,), (1,)), ((), ())), preferred_element_type=jnp.float32
        )
        inv_rms = rms[here, :]
        x_hat = acts[here, :].astype(jnp.float32) * inv_rms
        scaled = back * gain[...]
        mean = jnp.sum(scaled * x_hat, -1, keepdims=True) * (1.0 / width)
        layer_grad = (grad.astype(jnp.float32) + inv_rms * (scaled - x_hat * mean)).astype(
            jnp.bfloat16
        )
        out[...] = layer_grad
        din[here, :] = layer_grad
        acc[...] += jnp.sum((back * x_hat).reshape(rows // 8, 8, width), 0)


def in_vmem(value):
    return pltpu.with_memory_space_constraint(value, pltpu.VMEM)


whole = pl.BlockSpec(memory_space=pltpu.VMEM)


def chain_step(step, place, recv, weight, acts, rms, gain, grads, din, acc):
    rows, width = recv.shape
    return pl.pallas_call(
        functools.partial(step_kernel, step, acts.shape[0] // rows - 1),
        out_shape=(
            pltpu.VMEM((rows, width), jnp.bfloat16),
            pltpu.VMEM(grads.shape, grads.dtype),
            pltpu.VMEM(din.shape, din.dtype),
            pltpu.VMEM(acc.shape, acc.dtype),
        ),
        in_specs=[pl.BlockSpec(memory_space=pltpu.SMEM)] + [whole] * 8,
        out_specs=(whole,) * 4,
        input_output_aliases={6: 1, 7: 2, 8: 3},
        compiler_params=pltpu.CompilerParams(vmem_limit_bytes=8 * 2**20),
        cost_estimate=pl.CostEstimate(
            flops=2 * rows * width * width, bytes_accessed=width * width * 2, transcendentals=0
        ),
        name="chain_step",
    )(place, *[in_vmem(v) for v in (recv, weight, acts, rms, gain, grads, din, acc)])


def finish_kernel(normed_t, grads, din, acc, product, din_out, gain_out, slots, sems, din_sem):
    keep = pltpu.make_async_copy(din, din_out, din_sem)
    keep.start()
    gain_out[...] = jnp.sum(acc[...], 0, keepdims=True)
    rows = slots.shape[1]
    copies = []
    for block in range(product.shape[0] // rows):
        slot = block % 2
        if block >= 2:
            copies[block - 2].wait()
        slots[slot] = jnp.dot(
            normed_t[block * rows : (block + 1) * rows, :],
            grads[...],
            preferred_element_type=jnp.float32,
        ).astype(jnp.bfloat16)
        copies.append(
            pltpu.make_async_copy(
                slots.at[slot], product.at[block * rows : (block + 1) * rows, :], sems.at[slot]
            )
        )
        copies[-1].start()
    copies[-2].wait()
    copies[-1].wait()
    keep.wait()


def finish(normed_t, grads, din, acc):
    width, tokens = normed_t.shape
    anywhere = pl.BlockSpec(memory_space=pl.ANY)
    return pl.pallas_call(
        finish_kernel,
        out_shape=(
            pltpu.HBM((width, width), jnp.bfloat16),
            pltpu.HBM((tokens, width), jnp.bfloat16),
            jax.ShapeDtypeStruct((1, width), jnp.float32),
        ),
        in_specs=[whole] * 4,
        out_specs=(anywhere, anywhere, whole),
        scratch_shapes=[
            pltpu.VMEM((2, 256, width), jnp.bfloat16),
            pltpu.SemaphoreType.DMA((2,)),
            pltpu.SemaphoreType.DMA,
        ],
        compiler_params=pltpu.CompilerParams(vmem_limit_bytes=12 * 2**20),
        cost_estimate=pl.CostEstimate(
            flops=2 * tokens * width * width, bytes_accessed=width * width * 2, transcendentals=0
        ),
        name="finish",
    )(*[in_vmem(v) for v in (normed_t, grads, din, acc)])


def top_grads(layer_in, normed, weight, head, segs, labels):
    batches, rows = segs.shape
    width = layer_in.shape[1]
    cands = labels.shape[1]
    classes = head.shape[1]
    onehot = (segs[:, None, :] == jnp.arange(cands, dtype=jnp.int32)[None, :, None]).astype(
        jnp.bfloat16
    )
    counts = jnp.sum(onehot.astype(jnp.float32), -1).reshape(-1, 1)

    def pool(value):
        return jnp.einsum(
            "mcr,mrd->mcd",
            onehot,
            value.reshape(batches, rows, width),
            preferred_element_type=jnp.float32,
        ).reshape(-1, width)

    pooled_normed = pool(normed)
    high = lax.reduce_precision(pooled_normed, 8, 7)
    low = pooled_normed - high
    both = jnp.concatenate([high, low]).astype(jnp.bfloat16)
    product = jnp.dot(both, weight, preferred_element_type=jnp.float32)
    y_pool = pool(layer_in) + product[: batches * cands] + product[batches * cands :]
    pooled = (y_pool / counts).astype(jnp.bfloat16)
    logits = jnp.dot(pooled, head, preferred_element_type=jnp.float32)
    target = (
        labels.reshape(-1)[:, None] == jnp.arange(classes, dtype=jnp.int32)[None, :]
    ).astype(jnp.float32)
    dlogit = (jax.nn.sigmoid(logits) - target).astype(jnp.bfloat16)
    dpool = lax.dot_general(
        dlogit, head, (((1,), (1,)), ((), ())), preferred_element_type=jnp.float32
    )
    cand_grad = (dpool / counts).astype(jnp.bfloat16).reshape(batches, cands, width)
    return (
        jnp.einsum("mcr,mcd->mrd", onehot, cand_grad, preferred_element_type=jnp.float32)
        .astype(jnp.bfloat16)
        .reshape(-1, width)
    )


def per_device(acts, gains, proj, head, segs, labels):
    layer_in = acts[0]
    gain = gains[0]
    sections = lax.axis_size("section")
    section_pos = lax.axis_index("section")
    tokens, width = layer_in.shape
    weight = lax.all_gather(proj[0], "fsdp", axis=0, tiled=True)
    x_float = layer_in.astype(jnp.float32)
    inv_rms = lax.rsqrt(jnp.mean(x_float * x_float, -1, keepdims=True) + norm_eps)
    normed = (x_float * inv_rms * gain).astype(jnp.bfloat16)
    grads = top_grads(layer_in, normed, weight, head, segs, labels)

    pieces = tokens // piece
    place = jnp.reshape(sections - 1 - section_pos, (1,)).astype(jnp.int32)
    din = jnp.zeros((tokens, width), jnp.bfloat16)
    acc = jnp.zeros((8, width), jnp.float32)
    received = {}
    blank = jnp.zeros((piece, width), jnp.bfloat16)
    for step in range(pieces + lag * (sections - 1)):
        out, grads, din, acc = chain_step(
            step,
            place,
            received.pop(step - lag, blank),
            weight,
            layer_in,
            inv_rms,
            gain[None],
            grads,
            din,
            acc,
        )
        pairs = [
            (s, s - 1)
            for s in range(1, sections)
            if 0 <= step - lag * (sections - 1 - s) < pieces
        ]
        if pairs:
            received[step] = lax.ppermute(out, "section", pairs)

    product, din, gain_part = finish(normed.T, grads, din, acc)
    gain_total = lax.psum(gain_part[0], "fsdp")
    weight_part = lax.psum_scatter(product, "fsdp", scatter_dimension=0, tiled=True)
    return (din[None], weight_part[None], gain_total[None])


def solution(mesh):
    return jax.shard_map(
        per_device,
        mesh=mesh,
        in_specs=(
            P("section", "fsdp", None),
            P("section", None),
            P("section", "fsdp", None),
            P(),
            P("fsdp", None),
            P("fsdp", None),
        ),
        out_specs=(P("section", "fsdp", None), P("section", "fsdp", None), P("section", None)),
        check_vma=False,
    )
```

```python
import functools

import jax
import jax.numpy as jnp
from jax import lax
from jax.experimental import pallas as pl
from jax.experimental.pallas import tpu as pltpu
from jax.sharding import PartitionSpec as P

norm_eps = 1e-06
piece = 48
lag = 2
merged = 4
extra = 16


def step_kernel(
    step,
    last,
    place,
    recv,
    weight,
    acts,
    rms,
    gain,
    grads_in,
    din_in,
    acc_in,
    out,
    grads,
    din,
    acc,
    back,
):
    rows, width = recv.shape
    index = step - lag * place[0]

    @pl.when((index >= 0) & (index <= last))
    def _():
        row = pl.multiple_of(index * rows, 16)
        here = pl.ds(row, rows)

        @pl.when(place[0] > 0)
        def _():
            grads[here, :] = recv[...]

        grad = grads[here, :]
        inv_rms = rms[here, :]
        partial = jnp.zeros((rows, 128), jnp.float32)
        for pair in range(width // 256):
            columns = slice(pair * 256, (pair + 1) * 256)
            block = jnp.dot(
                grad,
                jnp.concatenate([weight[2 * pair], weight[2 * pair + 1]], axis=1),
                preferred_element_type=jnp.float32,
            )
            back[:, columns] = block
            along = block * (acts[here, columns].astype(jnp.float32) * inv_rms)
            acc[:, columns] += jnp.sum(along.reshape(rows // extra, extra, 256), 0)
            along = along * gain[:, columns]
            partial = partial + along[:, :128] + along[:, 128:]
        mean = jnp.sum(partial, -1, keepdims=True) * (1.0 / width)
        x_hat = acts[here, :].astype(jnp.float32) * inv_rms
        layer_grad = (
            grad.astype(jnp.float32) + inv_rms * (back[...] * gain[...] - x_hat * mean)
        ).astype(jnp.bfloat16)
        out[...] = layer_grad
        din[here, :] = layer_grad


def in_vmem(value):
    return pltpu.with_memory_space_constraint(value, pltpu.VMEM)


whole = pl.BlockSpec(memory_space=pltpu.VMEM)


def chain_step(step, place, recv, weight, acts, rms, gain, grads, din, acc):
    rows, width = recv.shape
    return pl.pallas_call(
        functools.partial(step_kernel, step, acts.shape[0] // rows - 1),
        out_shape=(
            pltpu.VMEM((rows, width), jnp.bfloat16),
            pltpu.VMEM(grads.shape, grads.dtype),
            pltpu.VMEM(din.shape, din.dtype),
            pltpu.VMEM(acc.shape, acc.dtype),
        ),
        in_specs=[pl.BlockSpec(memory_space=pltpu.SMEM)] + [whole] * 8,
        out_specs=(whole,) * 4,
        input_output_aliases={6: 1, 7: 2, 8: 3},
        scratch_shapes=[pltpu.VMEM((rows, width), jnp.float32)],
        compiler_params=pltpu.CompilerParams(vmem_limit_bytes=8 * 2**20),
        cost_estimate=pl.CostEstimate(
            flops=2 * rows * width * width, bytes_accessed=width * width * 2, transcendentals=0
        ),
        name="chain_step",
    )(place, *[in_vmem(v) for v in (recv, weight, acts, rms, gain, grads, din, acc)])


def finish_kernel(
    normed_t, grads, din, acc, product, din_out, slots, gain_slot, sems, gain_sem, din_sem
):
    devices, tall, width = product.shape
    rows = tall - extra
    keep = pltpu.make_async_copy(din, din_out, din_sem)
    keep.start()
    gain_slot[...] = acc[...].astype(jnp.bfloat16)
    gain_copies = [
        pltpu.make_async_copy(gain_slot, product.at[d, rows:, :], gain_sem.at[d])
        for d in range(devices)
    ]
    for copy in gain_copies:
        copy.start()
    copies = []
    for d in range(0, devices, 2):
        if d >= 4:
            copies[d - 4].wait()
            copies[d - 3].wait()
        block = jnp.dot(
            normed_t[d * rows : (d + 2) * rows, :],
            grads[...],
            preferred_element_type=jnp.float32,
        ).astype(jnp.bfloat16)
        for half in range(2):
            slot = (d + half) % 4
            slots[slot] = block[half * rows : (half + 1) * rows]
            copies.append(
                pltpu.make_async_copy(
                    slots.at[slot], product.at[d + half, :rows, :], sems.at[slot]
                )
            )
            copies[-1].start()
    for copy in copies[-4:] + gain_copies + [keep]:
        copy.wait()


def finish(normed_t, grads, din, acc, devices):
    width, tokens = normed_t.shape
    rows = width // devices
    anywhere = pl.BlockSpec(memory_space=pl.ANY)
    return pl.pallas_call(
        finish_kernel,
        out_shape=(
            pltpu.HBM((devices, rows + extra, width), jnp.bfloat16),
            pltpu.HBM((tokens, width), jnp.bfloat16),
        ),
        in_specs=[whole] * 4,
        out_specs=(anywhere, anywhere),
        scratch_shapes=[
            pltpu.VMEM((4, rows, width), jnp.bfloat16),
            pltpu.VMEM((extra, width), jnp.bfloat16),
            pltpu.SemaphoreType.DMA((4,)),
            pltpu.SemaphoreType.DMA((devices,)),
            pltpu.SemaphoreType.DMA,
        ],
        compiler_params=pltpu.CompilerParams(vmem_limit_bytes=12 * 2**20),
        cost_estimate=pl.CostEstimate(
            flops=2 * tokens * width * width, bytes_accessed=width * width * 2, transcendentals=0
        ),
        name="finish",
    )(*[in_vmem(v) for v in (normed_t, grads, din, acc)])


def flip_kernel(block, out):
    out[...] = block[...].T


def flip(block):
    return pl.pallas_call(
        flip_kernel,
        out_shape=jax.ShapeDtypeStruct(block.shape[::-1], block.dtype),
        in_specs=[whole],
        out_specs=whole,
        name="flip",
    )(block)


def top_kernel(
    gathered,
    head_in,
    both,
    pool_in,
    counts,
    labels,
    spread,
    weight,
    grads,
    product,
    head,
    sems,
    head_sem,
):
    devices = gathered.shape[0]
    head_copy = pltpu.make_async_copy(head_in, head, head_sem)
    copies = [
        pltpu.make_async_copy(gathered.at[d], weight.at[d], sems.at[d]) for d in range(devices)
    ]
    for copy in copies:
        copy.start()
    head_copy.start()
    for d in range(0, devices, 2):
        copies[d].wait()
        copies[d + 1].wait()
        part = lax.dot_general(
            both[:, d * 128 : (d + 2) * 128],
            jnp.concatenate([weight[d], weight[d + 1]], axis=1),
            (((1,), (1,)), ((), ())),
            preferred_element_type=jnp.float32,
        )
        product[...] = part if d == 0 else product[...] + part
    cands = counts.shape[0]
    y_pool = pool_in[...] + product[:cands, :] + product[cands:, :]
    pooled = (y_pool / counts[...]).astype(jnp.bfloat16)
    head_copy.wait()
    logits = jnp.dot(pooled, head[...], preferred_element_type=jnp.float32)
    classes = lax.broadcasted_iota(jnp.int32, logits.shape, 1)
    target = (labels[...] == classes).astype(jnp.float32)
    dlogit = (jax.nn.sigmoid(logits) - target).astype(jnp.bfloat16)
    dpool = lax.dot_general(
        dlogit, head[...], (((1,), (1,)), ((), ())), preferred_element_type=jnp.float32
    )
    cand_grad = (dpool / counts[...]).astype(jnp.bfloat16)
    grads[...] = jnp.dot(
        spread[...], cand_grad, preferred_element_type=jnp.float32
    ).astype(jnp.bfloat16)


def top_grads(layer_in, normed, gathered, head, segs, labels):
    batches, rows = segs.shape
    width = layer_in.shape[1]
    cands = labels.shape[1]
    onehot = (segs[:, None, :] == jnp.arange(cands, dtype=jnp.int32)[None, :, None]).astype(
        jnp.bfloat16
    )
    counts = jnp.sum(onehot.astype(jnp.float32), -1).reshape(-1, 1)
    owner = (segs + cands * jnp.arange(batches, dtype=jnp.int32)[:, None]).reshape(-1, 1)
    spread = (owner == jnp.arange(batches * cands, dtype=jnp.int32)[None]).astype(jnp.bfloat16)

    def pool(value):
        return jnp.einsum(
            "mcr,mrd->mcd",
            onehot,
            value.reshape(batches, rows, width),
            preferred_element_type=jnp.float32,
        ).reshape(-1, width)

    pooled_normed = pool(normed)
    high = lax.reduce_precision(pooled_normed, 8, 7)
    low = pooled_normed - high
    both = jnp.concatenate([high, low]).astype(jnp.bfloat16)
    devices = gathered.shape[0]
    return pl.pallas_call(
        top_kernel,
        out_shape=(
            pltpu.VMEM(gathered.shape, gathered.dtype),
            pltpu.VMEM(layer_in.shape, jnp.bfloat16),
        ),
        in_specs=[pl.BlockSpec(memory_space=pltpu.HBM)] * 2 + [whole] * 5,
        out_specs=(whole, whole),
        scratch_shapes=[
            pltpu.VMEM((2 * batches * cands, width), jnp.float32),
            pltpu.VMEM(head.shape, head.dtype),
            pltpu.SemaphoreType.DMA((devices,)),
            pltpu.SemaphoreType.DMA,
        ],
        compiler_params=pltpu.CompilerParams(vmem_limit_bytes=16 * 2**20),
        cost_estimate=pl.CostEstimate(
            flops=4 * batches * cands * width * width,
            bytes_accessed=width * width * 2,
            transcendentals=0,
        ),
        name="top",
    )(
        pltpu.with_memory_space_constraint(gathered, pltpu.HBM),
        pltpu.with_memory_space_constraint(head, pltpu.HBM),
        both,
        pool(layer_in),
        counts,
        labels.reshape(-1, 1),
        spread,
    )


def per_device(acts, gains, proj, head, segs, labels):
    layer_in = acts[0]
    gain = gains[0]
    sections = lax.axis_size("section")
    section_pos = lax.axis_index("section")
    tokens, width = layer_in.shape
    gathered = lax.all_gather(flip(proj[0]), "fsdp")
    x_float = layer_in.astype(jnp.float32)
    inv_rms = lax.rsqrt(jnp.mean(x_float * x_float, -1, keepdims=True) + norm_eps)
    normed = (x_float * inv_rms * gain).astype(jnp.bfloat16)
    weight, grads = top_grads(layer_in, normed, gathered, head, segs, labels)

    pieces = tokens // piece
    place = jnp.reshape(sections - 1 - section_pos, (1,)).astype(jnp.int32)
    din = jnp.zeros((tokens, width), jnp.bfloat16)
    acc = jnp.zeros((extra, width), jnp.float32)
    received = {}
    blank = jnp.zeros((piece, width), jnp.bfloat16)
    for step in range(pieces + lag * (sections - 1)):
        out, grads, din, acc = chain_step(
            step,
            place,
            received.pop(step - lag, blank),
            weight,
            layer_in,
            inv_rms,
            gain[None],
            grads,
            din,
            acc,
        )
        pairs = [
            (s, s - 1)
            for s in range(1, sections)
            if any(
                0 <= near - lag * (sections - 1 - s) < pieces
                for near in range(step - step % merged, step - step % merged + merged)
            )
        ]
        if pairs:
            received[step] = lax.ppermute(out, "section", pairs)

    product, din = finish(normed.T, grads, din, acc, lax.axis_size("fsdp"))
    summed = lax.psum_scatter(product, "fsdp", scatter_dimension=0)
    own = proj.shape[1]
    weight_part = summed[:own]
    gain_total = jnp.sum(summed[own:].astype(jnp.float32), 0)
    return (din[None], weight_part[None], gain_total[None])


def solution(mesh):
    return jax.shard_map(
        per_device,
        mesh=mesh,
        in_specs=(
            P("section", "fsdp", None),
            P("section", None),
            P("section", "fsdp", None),
            P(),
            P("fsdp", None),
            P("fsdp", None),
        ),
        out_specs=(P("section", "fsdp", None), P("section", "fsdp", None), P("section", None)),
        check_vma=False,
    )
```

```python
import functools

import jax
import jax.numpy as jnp
from jax import lax
from jax.experimental import pallas as pl
from jax.experimental.pallas import tpu as pltpu
from jax.sharding import PartitionSpec as P

norm_eps = 1e-06
piece = 48
lag = 2
merged = 6
ring = 4
extra = 16


def step_kernel(
    step,
    last,
    place,
    recv,
    weight,
    acts,
    rms,
    gain,
    grads_in,
    din_in,
    acc_in,
    out,
    grads,
    din,
    acc,
    back,
):
    rows, width = recv.shape
    index = step - lag * place[0]

    @pl.when((index >= 0) & (index <= last))
    def _():
        row = pl.multiple_of(index * rows, 16)
        here = pl.ds(row, rows)

        @pl.when(place[0] > 0)
        def _():
            grads[here, :] = recv[...]

        grad = grads[here, :]
        inv_rms = rms[here, :]
        partial = jnp.zeros((rows, 128), jnp.float32)
        for pair in range(width // 256):
            columns = slice(pair * 256, (pair + 1) * 256)
            block = jnp.dot(
                grad,
                jnp.concatenate([weight[2 * pair], weight[2 * pair + 1]], axis=1),
                preferred_element_type=jnp.float32,
            )
            back[:, columns] = block
            along = block * (acts[here, columns].astype(jnp.float32) * inv_rms)
            acc[:, columns] += jnp.sum(along.reshape(rows // extra, extra, 256), 0)
            along = along * gain[:, columns]
            partial = partial + along[:, :128] + along[:, 128:]
        mean = jnp.sum(partial, -1, keepdims=True) * (1.0 / width)
        x_hat = acts[here, :].astype(jnp.float32) * inv_rms
        layer_grad = (
            grad.astype(jnp.float32) + inv_rms * (back[...] * gain[...] - x_hat * mean)
        ).astype(jnp.bfloat16)
        out[...] = layer_grad
        din[here, :] = layer_grad


def in_vmem(value):
    return pltpu.with_memory_space_constraint(value, pltpu.VMEM)


whole = pl.BlockSpec(memory_space=pltpu.VMEM)


def chain_step(step, place, recv, weight, acts, rms, gain, grads, din, acc):
    rows, width = recv.shape
    return pl.pallas_call(
        functools.partial(step_kernel, step, acts.shape[0] // rows - 1),
        out_shape=(
            pltpu.VMEM((rows, width), jnp.bfloat16),
            pltpu.VMEM(grads.shape, grads.dtype),
            pltpu.VMEM(din.shape, din.dtype),
            pltpu.VMEM(acc.shape, acc.dtype),
        ),
        in_specs=[pl.BlockSpec(memory_space=pltpu.SMEM)] + [whole] * 8,
        out_specs=(whole,) * 4,
        input_output_aliases={6: 1, 7: 2, 8: 3},
        scratch_shapes=[pltpu.VMEM((rows, width), jnp.float32)],
        compiler_params=pltpu.CompilerParams(vmem_limit_bytes=8 * 2**20),
        cost_estimate=pl.CostEstimate(
            flops=2 * rows * width * width, bytes_accessed=width * width * 2, transcendentals=0
        ),
        name="chain_step",
    )(place, *[in_vmem(v) for v in (recv, weight, acts, rms, gain, grads, din, acc)])


def share_kernel(other, across, turns, place, normed_t, grads, acc, *rest):
    outs = rest[len(rest) - len(turns) :]
    arrived = rest[: len(rest) - len(turns)]
    rows = outs[0].shape[1] - extra
    along_x, along_y, core = place[1], place[2], place[3]
    slot = 0
    for out, group in zip(outs, turns):
        for position, turn in enumerate(group):
            block = (
                (along_x ^ across) * (2 * ring)
                + lax.rem(along_y + turn, ring) * 2
                + (core ^ other)
            )
            value = jnp.dot(
                normed_t[pl.ds(pl.multiple_of(block * rows, rows), rows), :],
                grads[...],
                preferred_element_type=jnp.float32,
            )
            gain_rows = acc[...]
            if arrived:
                value = value + arrived[0][slot, :rows, :].astype(jnp.float32)
                gain_rows = gain_rows + arrived[0][slot, rows:, :].astype(jnp.float32)
            out[position, :rows, :] = value.astype(jnp.bfloat16)
            out[position, rows:, :] = gain_rows.astype(jnp.bfloat16)
            slot += 1


def share(other, across, turns, place, normed_t, grads, acc, *arrived):
    width, tokens = normed_t.shape
    rows = width // (4 * ring) + extra
    return pl.pallas_call(
        functools.partial(share_kernel, other, across, turns),
        out_shape=tuple(
            pltpu.VMEM((len(group), rows, width), jnp.bfloat16) for group in turns
        ),
        in_specs=[pl.BlockSpec(memory_space=pltpu.SMEM)] + [whole] * (3 + len(arrived)),
        out_specs=(whole,) * len(turns),
        compiler_params=pltpu.CompilerParams(vmem_limit_bytes=8 * 2**20),
        cost_estimate=pl.CostEstimate(
            flops=tokens * width * width // 2, bytes_accessed=width * width, transcendentals=0
        ),
        name="share",
    )(place, *[in_vmem(v) for v in (normed_t, grads, acc) + arrived])


def add_far_kernel(own, arrived, left, right):
    half = left.shape[2]
    total = own[...].astype(jnp.float32) + arrived[...].astype(jnp.float32)
    left[...] = total[:, :, :half].astype(jnp.bfloat16)
    right[...] = total[:, :, half:].astype(jnp.bfloat16)


def add_near_kernel(own, arrived, from_before, from_after, after, before):
    half = from_before.shape[2]

    def total(which, columns):
        return own[which, :, columns].astype(jnp.float32) + arrived[which, :, columns].astype(
            jnp.float32
        )

    low, high = slice(0, half), slice(half, 2 * half)
    after[0, :, low] = (total(0, low) + from_before[0].astype(jnp.float32)).astype(jnp.bfloat16)
    after[0, :, high] = total(0, high).astype(jnp.bfloat16)
    before[0, :, low] = total(1, low).astype(jnp.bfloat16)
    before[0, :, high] = (total(1, high) + from_after[0].astype(jnp.float32)).astype(
        jnp.bfloat16
    )


def add_last_kernel(own, arrived, from_before, from_after, product, gain_sum):
    total = (own[0].astype(jnp.float32) + arrived[0].astype(jnp.float32)) + (
        from_before[0].astype(jnp.float32) + from_after[0].astype(jnp.float32)
    )
    rows = product.shape[0]
    product[...] = total[:rows].astype(jnp.bfloat16)
    gain_sum[...] = jnp.sum(total[rows:], 0, keepdims=True)


def add_call(kernel, out_shape, name, *values):
    return pl.pallas_call(
        kernel,
        out_shape=out_shape,
        in_specs=[whole] * len(values),
        out_specs=(whole,) * len(out_shape),
        compiler_params=pltpu.CompilerParams(vmem_limit_bytes=8 * 2**20),
        name=name,
    )(*[in_vmem(v) for v in values])


def fsdp_move(value, dx=0, dy=0, dc=0):
    pairs = []
    for x in range(2):
        for y in range(ring):
            for c in range(2):
                target = ((x + dx) % 2 * ring + (y + dy) % ring) * 2 + (c + dc) % 2
                pairs.append(((x * ring + y) * 2 + c, target))
    return lax.ppermute(value, "fsdp", pairs)


def scatter_sum(place, normed_t, grads, acc, own_rows):
    width = normed_t.shape[0]
    whole_turn = ((2, 1, 3, 0),)
    far_other = share(1, 1, whole_turn, place, normed_t, grads, acc)[0]
    far_arrived = fsdp_move(far_other, dc=1)
    near_other = share(1, 0, whole_turn, place, normed_t, grads, acc)[0]
    near_arrived = fsdp_move(near_other, dc=1)
    split_turns = ((2,), (1, 3), (0,))
    far_two, far_side, far_same = share(
        0, 1, split_turns, place, normed_t, grads, acc, far_arrived
    )
    far_two = fsdp_move(far_two, dx=1)
    far_side = fsdp_move(far_side, dx=1)
    far_same = fsdp_move(far_same, dx=1)
    near_two, near_side, near_same = share(
        0, 0, split_turns, place, normed_t, grads, acc, near_arrived
    )
    rows = near_two.shape[1]
    half = pltpu.VMEM((1, rows, width // 2), jnp.bfloat16)
    one = pltpu.VMEM((1, rows, width), jnp.bfloat16)
    left, right = add_call(add_far_kernel, (half, half), "add_far", near_two, far_two)
    from_before = fsdp_move(left, dy=1)
    from_after = fsdp_move(right, dy=-1)
    after, before = add_call(
        add_near_kernel, (one, one), "add_near", near_side, far_side, from_before, from_after
    )
    from_before = fsdp_move(after, dy=1)
    from_after = fsdp_move(before, dy=-1)
    return add_call(
        add_last_kernel,
        (
            jax.ShapeDtypeStruct((own_rows, width), jnp.bfloat16),
            jax.ShapeDtypeStruct((1, width), jnp.float32),
        ),
        "add_last",
        near_same,
        far_same,
        from_before,
        from_after,
    )


def flip_kernel(block, out):
    out[...] = block[...].T


def flip(block):
    return pl.pallas_call(
        flip_kernel,
        out_shape=jax.ShapeDtypeStruct(block.shape[::-1], block.dtype),
        in_specs=[whole],
        out_specs=whole,
        name="flip",
    )(block)


def top_kernel(
    gathered,
    head_in,
    both,
    pool_in,
    counts,
    labels,
    spread,
    weight,
    grads,
    product,
    head,
    sems,
    head_sem,
):
    devices = gathered.shape[0]
    head_copy = pltpu.make_async_copy(head_in, head, head_sem)
    copies = [
        pltpu.make_async_copy(gathered.at[d], weight.at[d], sems.at[d]) for d in range(devices)
    ]
    for copy in copies:
        copy.start()
    head_copy.start()
    for d in range(0, devices, 2):
        copies[d].wait()
        copies[d + 1].wait()
        part = lax.dot_general(
            both[:, d * 128 : (d + 2) * 128],
            jnp.concatenate([weight[d], weight[d + 1]], axis=1),
            (((1,), (1,)), ((), ())),
            preferred_element_type=jnp.float32,
        )
        product[...] = part if d == 0 else product[...] + part
    cands = counts.shape[0]
    y_pool = pool_in[...] + product[:cands, :] + product[cands:, :]
    pooled = (y_pool / counts[...]).astype(jnp.bfloat16)
    head_copy.wait()
    logits = jnp.dot(pooled, head[...], preferred_element_type=jnp.float32)
    classes = lax.broadcasted_iota(jnp.int32, logits.shape, 1)
    target = (labels[...] == classes).astype(jnp.float32)
    dlogit = (jax.nn.sigmoid(logits) - target).astype(jnp.bfloat16)
    dpool = lax.dot_general(
        dlogit, head[...], (((1,), (1,)), ((), ())), preferred_element_type=jnp.float32
    )
    cand_grad = (dpool / counts[...]).astype(jnp.bfloat16)
    grads[...] = jnp.dot(
        spread[...], cand_grad, preferred_element_type=jnp.float32
    ).astype(jnp.bfloat16)


def top_grads(layer_in, normed, gathered, head, segs, labels):
    batches, rows = segs.shape
    width = layer_in.shape[1]
    cands = labels.shape[1]
    onehot = (segs[:, None, :] == jnp.arange(cands, dtype=jnp.int32)[None, :, None]).astype(
        jnp.bfloat16
    )
    counts = jnp.sum(onehot.astype(jnp.float32), -1).reshape(-1, 1)
    owner = (segs + cands * jnp.arange(batches, dtype=jnp.int32)[:, None]).reshape(-1, 1)
    spread = (owner == jnp.arange(batches * cands, dtype=jnp.int32)[None]).astype(jnp.bfloat16)

    def pool(value):
        return jnp.einsum(
            "mcr,mrd->mcd",
            onehot,
            value.reshape(batches, rows, width),
            preferred_element_type=jnp.float32,
        ).reshape(-1, width)

    pooled_normed = pool(normed)
    high = lax.reduce_precision(pooled_normed, 8, 7)
    low = pooled_normed - high
    both = jnp.concatenate([high, low]).astype(jnp.bfloat16)
    devices = gathered.shape[0]
    return pl.pallas_call(
        top_kernel,
        out_shape=(
            pltpu.VMEM(gathered.shape, gathered.dtype),
            pltpu.VMEM(layer_in.shape, jnp.bfloat16),
        ),
        in_specs=[pl.BlockSpec(memory_space=pltpu.HBM)] * 2 + [whole] * 5,
        out_specs=(whole, whole),
        scratch_shapes=[
            pltpu.VMEM((2 * batches * cands, width), jnp.float32),
            pltpu.VMEM(head.shape, head.dtype),
            pltpu.SemaphoreType.DMA((devices,)),
            pltpu.SemaphoreType.DMA,
        ],
        compiler_params=pltpu.CompilerParams(vmem_limit_bytes=16 * 2**20),
        cost_estimate=pl.CostEstimate(
            flops=4 * batches * cands * width * width,
            bytes_accessed=width * width * 2,
            transcendentals=0,
        ),
        name="top",
    )(
        pltpu.with_memory_space_constraint(gathered, pltpu.HBM),
        pltpu.with_memory_space_constraint(head, pltpu.HBM),
        both,
        pool(layer_in),
        counts,
        labels.reshape(-1, 1),
        spread,
    )


def per_device(acts, gains, proj, head, segs, labels):
    layer_in = acts[0]
    gain = gains[0]
    sections = lax.axis_size("section")
    section_pos = lax.axis_index("section")
    tokens, width = layer_in.shape
    gathered = lax.all_gather(flip(proj[0]), "fsdp")
    x_float = layer_in.astype(jnp.float32)
    inv_rms = lax.rsqrt(jnp.mean(x_float * x_float, -1, keepdims=True) + norm_eps)
    normed = (x_float * inv_rms * gain).astype(jnp.bfloat16)
    weight, grads = top_grads(layer_in, normed, gathered, head, segs, labels)

    pieces = tokens // piece
    fsdp_pos = lax.axis_index("fsdp")
    place = jnp.stack(
        [sections - 1 - section_pos, fsdp_pos // (2 * ring), fsdp_pos // 2 % ring, fsdp_pos % 2]
    ).astype(jnp.int32)
    din = jnp.zeros((tokens, width), jnp.bfloat16)
    acc = jnp.zeros((extra, width), jnp.float32)
    received = {}
    blank = jnp.zeros((piece, width), jnp.bfloat16)
    for step in range(pieces + lag * (sections - 1)):
        out, grads, din, acc = chain_step(
            step,
            place,
            received.pop(step - lag, blank),
            weight,
            layer_in,
            inv_rms,
            gain[None],
            grads,
            din,
            acc,
        )
        pairs = [
            (s, s - 1)
            for s in range(1, sections)
            if any(
                0 <= near - lag * (sections - 1 - s) < pieces
                for near in range(step - step % merged, step - step % merged + merged)
            )
        ]
        if pairs:
            received[step] = lax.ppermute(out, "section", pairs)

    weight_part, gain_total = scatter_sum(place, normed.T, grads, acc, proj.shape[1])
    return (din[None], weight_part[None], gain_total)


def solution(mesh):
    return jax.shard_map(
        per_device,
        mesh=mesh,
        in_specs=(
            P("section", "fsdp", None),
            P("section", None),
            P("section", "fsdp", None),
            P(),
            P("fsdp", None),
            P("fsdp", None),
        ),
        out_specs=(P("section", "fsdp", None), P("section", "fsdp", None), P("section", None)),
        check_vma=False,
    )
```

```python
import functools

import jax
import jax.numpy as jnp
from jax import lax
from jax.experimental import pallas as pl
from jax.experimental.pallas import tpu as pltpu
from jax.sharding import PartitionSpec as P

norm_eps = 1e-06
piece = 48
lag = 2
merged = 4
ring = 4
extra = 16


def step_kernel(
    step,
    last,
    place,
    recv,
    weight,
    acts,
    rms,
    gain,
    grads_in,
    din_in,
    acc_in,
    out,
    grads,
    din,
    acc,
    back,
):
    rows, width = recv.shape
    index = step - lag * place[0]

    @pl.when((index >= 0) & (index <= last))
    def _():
        row = pl.multiple_of(index * rows, 16)
        here = pl.ds(row, rows)

        @pl.when(place[0] > 0)
        def _():
            grads[here, :] = recv[...]

        grad = grads[here, :]
        inv_rms = rms[here, :]
        partial = jnp.zeros((rows, 128), jnp.float32)
        for pair in range(width // 256):
            columns = slice(pair * 256, (pair + 1) * 256)
            block = jnp.dot(
                grad,
                jnp.concatenate([weight[2 * pair], weight[2 * pair + 1]], axis=1),
                preferred_element_type=jnp.float32,
            )
            back[:, columns] = block
            along = block * (acts[here, columns].astype(jnp.float32) * inv_rms)
            acc[:, columns] += jnp.sum(along.reshape(rows // extra, extra, 256), 0)
            along = along * gain[:, columns]
            partial = partial + along[:, :128] + along[:, 128:]
        mean = jnp.sum(partial, -1, keepdims=True) * (1.0 / width)
        x_hat = acts[here, :].astype(jnp.float32) * inv_rms
        layer_grad = (
            grad.astype(jnp.float32) + inv_rms * (back[...] * gain[...] - x_hat * mean)
        ).astype(jnp.bfloat16)
        out[...] = layer_grad
        din[here, :] = layer_grad


def in_vmem(value):
    return pltpu.with_memory_space_constraint(value, pltpu.VMEM)


whole = pl.BlockSpec(memory_space=pltpu.VMEM)


def chain_step(step, place, recv, weight, acts, rms, gain, grads, din, acc):
    rows, width = recv.shape
    return pl.pallas_call(
        functools.partial(step_kernel, step, acts.shape[0] // rows - 1),
        out_shape=(
            pltpu.VMEM((rows, width), jnp.bfloat16),
            pltpu.VMEM(grads.shape, grads.dtype),
            pltpu.VMEM(din.shape, din.dtype),
            pltpu.VMEM(acc.shape, acc.dtype),
        ),
        in_specs=[pl.BlockSpec(memory_space=pltpu.SMEM)] + [whole] * 8,
        out_specs=(whole,) * 4,
        input_output_aliases={6: 1, 7: 2, 8: 3},
        scratch_shapes=[pltpu.VMEM((rows, width), jnp.float32)],
        compiler_params=pltpu.CompilerParams(vmem_limit_bytes=8 * 2**20),
        cost_estimate=pl.CostEstimate(
            flops=2 * rows * width * width, bytes_accessed=width * width * 2, transcendentals=0
        ),
        name="chain_step",
    )(place, *[in_vmem(v) for v in (recv, weight, acts, rms, gain, grads, din, acc)])


def share_kernel(other, across, parts, place, normed_t, grads, acc, *rest):
    outs = rest[len(rest) - len(parts) :]
    arrived = rest[: len(rest) - len(parts)]
    rows = outs[0].shape[1] - extra
    along_x, along_y, core = place[1], place[2], place[3]
    for slot, turn in enumerate(turns):
        block = (
            (along_x ^ across) * (2 * ring) + lax.rem(along_y + turn, ring) * 2 + (core ^ other)
        )
        value = jnp.dot(
            normed_t[pl.ds(pl.multiple_of(block * rows, rows), rows), :],
            grads[...],
            preferred_element_type=jnp.float32,
        )
        gain_rows = acc[...]
        if arrived:
            value = value + arrived[0][slot, :rows, :].astype(jnp.float32)
            gain_rows = gain_rows + arrived[0][slot, rows:, :].astype(jnp.float32)
        value = value.astype(jnp.bfloat16)
        gain_rows = gain_rows.astype(jnp.bfloat16)
        for out, (held, start, stop) in zip(outs, parts):
            if turn in held:
                out[held.index(turn), :rows, :] = value[:, start:stop]
                out[held.index(turn), rows:, :] = gain_rows[:, start:stop]


def share(other, across, parts, place, normed_t, grads, acc, *arrived):
    width, tokens = normed_t.shape
    rows = width // (4 * ring) + extra
    return pl.pallas_call(
        functools.partial(share_kernel, other, across, parts),
        out_shape=tuple(
            pltpu.VMEM((len(held), rows, stop - start), jnp.bfloat16)
            for held, start, stop in parts
        ),
        in_specs=[pl.BlockSpec(memory_space=pltpu.SMEM)] + [whole] * (3 + len(arrived)),
        out_specs=(whole,) * len(parts),
        compiler_params=pltpu.CompilerParams(vmem_limit_bytes=8 * 2**20),
        cost_estimate=pl.CostEstimate(
            flops=tokens * width * width // 2, bytes_accessed=width * width, transcendentals=0
        ),
        name="share",
    )(place, *[in_vmem(v) for v in (normed_t, grads, acc) + arrived])


def wide(value):
    return value.astype(jnp.float32)


def add_two_kernel(own, arrived, left, right):
    half = left.shape[2]
    total = wide(own[0]) + wide(arrived[0])
    left[0] = total[:, :half].astype(jnp.bfloat16)
    right[0] = total[:, half:].astype(jnp.bfloat16)


def add_side_kernel(own, arrived, from_before, from_after, after, before):
    half = from_before.shape[2]
    up, down = wide(own[1]) + wide(arrived[0]), wide(own[2]) + wide(arrived[1])
    after[0, :, :half] = (up[:, :half] + wide(from_before[0])).astype(jnp.bfloat16)
    after[0, :, half:] = up[:, half:].astype(jnp.bfloat16)
    before[0, :, :half] = down[:, :half].astype(jnp.bfloat16)
    before[0, :, half:] = (down[:, half:] + wide(from_after[0])).astype(jnp.bfloat16)


def add_both_kernel(near, far, near_before, near_after, far_before, far_after, after, before):
    half = near_before.shape[2]
    for which, (own, low, high) in enumerate(
        ((near, near_before, near_after), (far, far_before, far_after))
    ):
        after[which, :, :half] = (wide(own[0, :, :half]) + wide(low[0])).astype(jnp.bfloat16)
        after[which, :, half:] = own[0, :, half:]
        before[which, :, :half] = own[1, :, :half]
        before[which, :, half:] = (wide(own[1, :, half:]) + wide(high[0])).astype(jnp.bfloat16)


def add_far_kernel(own, from_before, from_after, out):
    out[0] = (wide(own[0]) + (wide(from_before[1]) + wide(from_after[1]))).astype(jnp.bfloat16)


def add_last_kernel(
    low_own,
    low_arrived,
    low_before,
    low_after,
    high_own,
    high_before,
    high_after,
    high_arrived,
    product,
    gain_sum,
):
    rows, width = product.shape
    low = (wide(low_own[3]) + wide(low_arrived[2])) + (wide(low_before[0]) + wide(low_after[0]))
    high = (wide(high_own[0]) + wide(high_arrived[0])) + (
        wide(high_before[0]) + wide(high_after[0])
    )
    for total, columns in ((low, slice(0, width // 2)), (high, slice(width // 2, width))):
        product[:, columns] = total[:rows].astype(jnp.bfloat16)
        gain_sum[:, columns] = jnp.sum(total[rows:], 0, keepdims=True)


def add_call(kernel, out_shape, name, *values):
    return pl.pallas_call(
        kernel,
        out_shape=out_shape,
        in_specs=[whole] * len(values),
        out_specs=(whole,) * len(out_shape),
        compiler_params=pltpu.CompilerParams(vmem_limit_bytes=8 * 2**20),
        name=name,
    )(*[in_vmem(v) for v in values])


def fsdp_move(value, dx=0, dy=0, dc=0):
    pairs = []
    for x in range(2):
        for y in range(ring):
            for c in range(2):
                target = ((x + dx) % 2 * ring + (y + dy) % ring) * 2 + (c + dc) % 2
                pairs.append(((x * ring + y) * 2 + c, target))
    return lax.ppermute(value, "fsdp", pairs)


turns = (2, 1, 3, 0)


def scatter_sum(place, normed_t, grads, acc, own_rows):
    width = normed_t.shape[0]
    half, quarter = width // 2, width // 4
    everything = ((turns, 0, width),)
    high_parts = (
        ((2,), half, half + quarter),
        ((2,), half + quarter, width),
        ((1, 3), half, width),
        ((0,), half, width),
    )
    local = (normed_t, grads, acc)
    far_arrived = fsdp_move(share(1, 1, everything, place, *local)[0], dc=1)
    near_arrived = fsdp_move(share(1, 0, everything, place, *local)[0], dc=1)
    far_two, far_rest, far_left, far_right, far_side, far_same = share(
        0,
        1,
        (((2,), 0, half), ((1, 3, 0), 0, half)) + high_parts,
        place,
        *local,
        far_arrived,
    )
    far_two = fsdp_move(far_two, dx=1)
    far_before, far_after = fsdp_move(far_left, dy=1), fsdp_move(far_right, dy=-1)
    far_rest = fsdp_move(far_rest, dx=1)
    low, near_left, near_right, near_side, near_same = share(
        0, 0, ((turns, 0, half),) + high_parts, place, *local, near_arrived
    )
    near_before, near_after = fsdp_move(near_left, dy=1), fsdp_move(near_right, dy=-1)

    def shaped(count, columns):
        return pltpu.VMEM((count, low.shape[1], columns), jnp.bfloat16)

    after, before = add_call(
        add_both_kernel,
        (shaped(2, half),) * 2,
        "add_both",
        near_side,
        far_side,
        near_before,
        near_after,
        far_before,
        far_after,
    )
    high_before, high_after = fsdp_move(after, dy=1), fsdp_move(before, dy=-1)
    left, right = add_call(add_two_kernel, (shaped(1, quarter),) * 2, "add_two", low, far_two)
    from_before, from_after = fsdp_move(left, dy=1), fsdp_move(right, dy=-1)
    after, before = add_call(
        add_side_kernel,
        (shaped(1, half),) * 2,
        "add_side",
        low,
        far_rest,
        from_before,
        from_after,
    )
    low_before, low_after = fsdp_move(after, dy=1), fsdp_move(before, dy=-1)
    (far_sum,) = add_call(
        add_far_kernel, (shaped(1, half),), "add_far", far_same, high_before, high_after
    )
    high_arrived = fsdp_move(far_sum, dx=1)
    return add_call(
        add_last_kernel,
        (
            jax.ShapeDtypeStruct((own_rows, width), jnp.bfloat16),
            jax.ShapeDtypeStruct((1, width), jnp.float32),
        ),
        "add_last",
        low,
        far_rest,
        low_before,
        low_after,
        near_same,
        high_before,
        high_after,
        high_arrived,
    )


def flip_kernel(block, out):
    half = out.shape[1]
    out[0] = block[:, :half].T
    out[1] = block[:, half:].T


def flip(block):
    return pl.pallas_call(
        flip_kernel,
        out_shape=jax.ShapeDtypeStruct(
            (2, block.shape[1] // 2, block.shape[0]), block.dtype
        ),
        in_specs=[whole],
        out_specs=whole,
        name="flip",
    )(block)


def gather_weight(block):
    own = flip(block)
    below, above = fsdp_move(own, dy=1), fsdp_move(own, dy=-1)
    beside = fsdp_move(own, dx=1)
    up = fsdp_move(jnp.stack([below[0], beside[0]]), dy=1)
    down = fsdp_move(jnp.stack([above[1], beside[1]]), dy=-1)
    mixed = fsdp_move(jnp.stack([below[1], above[0]]), dx=1)
    last = fsdp_move(jnp.stack([up[0], down[0]]), dx=1)
    pieces = (own, below, above, beside, up, down, mixed, last)
    return pieces + tuple(fsdp_move(piece, dc=1) for piece in pieces)


sources = (
    (0, 0, ((0, 0), (0, 1))),
    (0, 3, ((1, 0), (1, 1))),
    (0, 1, ((2, 0), (2, 1))),
    (1, 0, ((3, 0), (3, 1))),
    (0, 2, ((4, 0), (5, 0))),
    (1, 3, ((4, 1), (6, 0))),
    (1, 1, ((6, 1), (5, 1))),
    (1, 2, ((7, 0), (7, 1))),
)


def top_kernel(place, *refs):
    received = refs[:16]
    head_in, both, pool_in, counts, labels, spread, weight, grads = refs[16:24]
    product, head, sems, head_sem = refs[24:]
    head_copy = pltpu.make_async_copy(head_in, head, head_sem)
    along_x, along_y, core = place[1], place[2], place[3]
    half = weight.shape[1] // 2
    chips, copies = [], []
    for order, (dx, dy, halves) in enumerate(sources):
        chip = (along_x ^ dx) * ring + lax.rem(along_y + dy, ring)
        chips.append(chip)
        copies.append(
            [
                pltpu.make_async_copy(
                    received[8 * dc + piece_index].at[which],
                    weight.at[2 * chip + (core ^ dc), part * half : (part + 1) * half, :],
                    sems.at[order, 2 * dc + part],
                )
                for dc in range(2)
                for part, (piece_index, which) in enumerate(halves)
            ]
        )
        for copy in copies[-1]:
            copy.start()
    head_copy.start()
    for order, chip in enumerate(chips):
        for copy in copies[order]:
            copy.wait()
        part = lax.dot_general(
            jnp.concatenate([both[2 * chip], both[2 * chip + 1]], axis=1),
            jnp.concatenate([weight[2 * chip], weight[2 * chip + 1]], axis=1),
            (((1,), (1,)), ((), ())),
            preferred_element_type=jnp.float32,
        )
        product[...] = part if order == 0 else product[...] + part
    cands = counts.shape[0]
    y_pool = pool_in[...] + product[:cands, :] + product[cands:, :]
    pooled = (y_pool / counts[...]).astype(jnp.bfloat16)
    head_copy.wait()
    logits = jnp.dot(pooled, head[...], preferred_element_type=jnp.float32)
    classes = lax.broadcasted_iota(jnp.int32, logits.shape, 1)
    target = (labels[...] == classes).astype(jnp.float32)
    dlogit = (jax.nn.sigmoid(logits) - target).astype(jnp.bfloat16)
    dpool = lax.dot_general(
        dlogit, head[...], (((1,), (1,)), ((), ())), preferred_element_type=jnp.float32
    )
    cand_grad = (dpool / counts[...]).astype(jnp.bfloat16)
    grads[...] = jnp.dot(
        spread[...], cand_grad, preferred_element_type=jnp.float32
    ).astype(jnp.bfloat16)


def top_grads(place, layer_in, normed, gathered, head, segs, labels):
    batches, rows = segs.shape
    width = layer_in.shape[1]
    cands = labels.shape[1]
    onehot = (segs[:, None, :] == jnp.arange(cands, dtype=jnp.int32)[None, :, None]).astype(
        jnp.bfloat16
    )
    counts = jnp.sum(onehot.astype(jnp.float32), -1).reshape(-1, 1)
    owner = (segs + cands * jnp.arange(batches, dtype=jnp.int32)[:, None]).reshape(-1, 1)
    spread = (owner == jnp.arange(batches * cands, dtype=jnp.int32)[None]).astype(jnp.bfloat16)

    def pool(value):
        return jnp.einsum(
            "mcr,mrd->mcd",
            onehot,
            value.reshape(batches, rows, width),
            preferred_element_type=jnp.float32,
        ).reshape(-1, width)

    pooled_normed = pool(normed)
    high = lax.reduce_precision(pooled_normed, 8, 7)
    low = pooled_normed - high
    both = jnp.concatenate([high, low]).astype(jnp.bfloat16)
    devices = 4 * ring
    both = both.reshape(-1, devices, width // devices).transpose(1, 0, 2)
    return pl.pallas_call(
        top_kernel,
        out_shape=(
            pltpu.VMEM((devices, width, width // devices), jnp.bfloat16),
            pltpu.VMEM(layer_in.shape, jnp.bfloat16),
        ),
        in_specs=[pl.BlockSpec(memory_space=pltpu.SMEM)]
        + [pl.BlockSpec(memory_space=pltpu.HBM)] * 17
        + [whole] * 5,
        out_specs=(whole, whole),
        scratch_shapes=[
            pltpu.VMEM((2 * batches * cands, width), jnp.float32),
            pltpu.VMEM(head.shape, head.dtype),
            pltpu.SemaphoreType.DMA((len(sources), 4)),
            pltpu.SemaphoreType.DMA,
        ],
        compiler_params=pltpu.CompilerParams(vmem_limit_bytes=16 * 2**20),
        cost_estimate=pl.CostEstimate(
            flops=4 * batches * cands * width * width,
            bytes_accessed=width * width * 2,
            transcendentals=0,
        ),
        name="top",
    )(
        place,
        *[pltpu.with_memory_space_constraint(v, pltpu.HBM) for v in gathered],
        pltpu.with_memory_space_constraint(head, pltpu.HBM),
        both,
        pool(layer_in),
        counts,
        labels.reshape(-1, 1),
        spread,
    )


def per_device(acts, gains, proj, head, segs, labels):
    layer_in = acts[0]
    gain = gains[0]
    sections = lax.axis_size("section")
    section_pos = lax.axis_index("section")
    tokens, width = layer_in.shape
    gathered = gather_weight(proj[0])
    x_float = layer_in.astype(jnp.float32)
    inv_rms = lax.rsqrt(jnp.mean(x_float * x_float, -1, keepdims=True) + norm_eps)
    normed = (x_float * inv_rms * gain).astype(jnp.bfloat16)
    fsdp_pos = lax.axis_index("fsdp")
    place = jnp.stack(
        [sections - 1 - section_pos, fsdp_pos // (2 * ring), fsdp_pos // 2 % ring, fsdp_pos % 2]
    ).astype(jnp.int32)
    weight, grads = top_grads(place, layer_in, normed, gathered, head, segs, labels)

    pieces = tokens // piece
    din = jnp.zeros((tokens, width), jnp.bfloat16)
    acc = jnp.zeros((extra, width), jnp.float32)
    received = {}
    blank = jnp.zeros((piece, width), jnp.bfloat16)
    for step in range(pieces + lag * (sections - 1)):
        out, grads, din, acc = chain_step(
            step,
            place,
            received.pop(step - lag, blank),
            weight,
            layer_in,
            inv_rms,
            gain[None],
            grads,
            din,
            acc,
        )
        pairs = [
            (s, s - 1)
            for s in range(1, sections)
            if any(
                0 <= near - lag * (sections - 1 - s) < pieces
                for near in range(step - step % merged, step - step % merged + merged)
            )
        ]
        if pairs:
            received[step] = lax.ppermute(out, "section", pairs)

    weight_part, gain_total = scatter_sum(place, normed.T, grads, acc, proj.shape[1])
    return (din[None], weight_part[None], gain_total)


def solution(mesh):
    return jax.shard_map(
        per_device,
        mesh=mesh,
        in_specs=(
            P("section", "fsdp", None),
            P("section", None),
            P("section", "fsdp", None),
            P(),
            P("fsdp", None),
            P("fsdp", None),
        ),
        out_specs=(P("section", "fsdp", None), P("section", "fsdp", None), P("section", None)),
        check_vma=False,
    )
```

```python
import functools

import jax
import jax.numpy as jnp
from jax import lax
from jax.experimental import pallas as pl
from jax.experimental.pallas import tpu as pltpu
from jax.sharding import PartitionSpec as P

norm_eps = 1e-06
piece = 48
lag = 3
merged = 7
ring = 4
extra = 16


def step_kernel(
    step,
    last,
    place,
    recv,
    weight,
    acts,
    rms,
    gain,
    grads_in,
    din_in,
    acc_in,
    out,
    grads,
    din,
    acc,
    back,
):
    rows, width = recv.shape
    index = step - lag * place[0]

    @pl.when((index >= 0) & (index <= last))
    def _():
        row = pl.multiple_of(index * rows, 16)
        here = pl.ds(row, rows)

        @pl.when(place[0] > 0)
        def _():
            grads[here, :] = recv[...]

        grad = grads[here, :]
        inv_rms = rms[here, :]
        partial = jnp.zeros((rows, 128), jnp.float32)
        for pair in range(width // 256):
            columns = slice(pair * 256, (pair + 1) * 256)
            block = jnp.dot(
                grad,
                jnp.concatenate([weight[2 * pair], weight[2 * pair + 1]], axis=1),
                preferred_element_type=jnp.float32,
            )
            back[:, columns] = block
            along = block * (acts[here, columns].astype(jnp.float32) * inv_rms)
            acc[:, columns] += jnp.sum(along.reshape(rows // extra, extra, 256), 0)
            along = along * gain[:, columns]
            partial = partial + along[:, :128] + along[:, 128:]
        mean = jnp.sum(partial, -1, keepdims=True) * (1.0 / width)
        x_hat = acts[here, :].astype(jnp.float32) * inv_rms
        layer_grad = (
            grad.astype(jnp.float32) + inv_rms * (back[...] * gain[...] - x_hat * mean)
        ).astype(jnp.bfloat16)
        out[...] = layer_grad
        din[here, :] = layer_grad


def in_vmem(value):
    return pltpu.with_memory_space_constraint(value, pltpu.VMEM)


whole = pl.BlockSpec(memory_space=pltpu.VMEM)


def chain_step(step, place, recv, weight, acts, rms, gain, grads, din, acc):
    rows, width = recv.shape
    return pl.pallas_call(
        functools.partial(step_kernel, step, acts.shape[0] // rows - 1),
        out_shape=(
            pltpu.VMEM((rows, width), jnp.bfloat16),
            pltpu.VMEM(grads.shape, grads.dtype),
            pltpu.VMEM(din.shape, din.dtype),
            pltpu.VMEM(acc.shape, acc.dtype),
        ),
        in_specs=[pl.BlockSpec(memory_space=pltpu.SMEM)] + [whole] * 8,
        out_specs=(whole,) * 4,
        input_output_aliases={6: 1, 7: 2, 8: 3},
        scratch_shapes=[pltpu.VMEM((rows, width), jnp.float32)],
        compiler_params=pltpu.CompilerParams(vmem_limit_bytes=8 * 2**20),
        cost_estimate=pl.CostEstimate(
            flops=2 * rows * width * width, bytes_accessed=width * width * 2, transcendentals=0
        ),
        name="chain_step",
    )(place, *[in_vmem(v) for v in (recv, weight, acts, rms, gain, grads, din, acc)])


def share_kernel(other, across, parts, at_x, at_y, at_core, normed_t, grads, acc, *rest):
    outs = rest[len(rest) - len(parts) :]
    arrived = rest[: len(rest) - len(parts)]
    rows = outs[0].shape[1] - extra
    along_x, along_y, core = at_x[0], at_y[0], at_core[0]
    for slot, turn in enumerate(turns):
        block = (
            (along_x ^ across) * (2 * ring) + lax.rem(along_y + turn, ring) * 2 + (core ^ other)
        )
        value = jnp.dot(
            normed_t[pl.ds(pl.multiple_of(block * rows, rows), rows), :],
            grads[...],
            preferred_element_type=jnp.float32,
        )
        gain_rows = acc[...]
        if arrived:
            value = value + arrived[0][slot, :rows, :].astype(jnp.float32)
            gain_rows = gain_rows + arrived[0][slot, rows:, :].astype(jnp.float32)
        value = value.astype(jnp.bfloat16)
        gain_rows = gain_rows.astype(jnp.bfloat16)
        for out, (held, start, stop) in zip(outs, parts):
            if turn in held:
                out[held.index(turn), :rows, :] = value[:, start:stop]
                out[held.index(turn), rows:, :] = gain_rows[:, start:stop]


def share(other, across, parts, place, normed_t, grads, acc, *arrived):
    width, tokens = normed_t.shape
    rows = width // (4 * ring) + extra
    return pl.pallas_call(
        functools.partial(share_kernel, other, across, parts),
        out_shape=tuple(
            pltpu.VMEM((len(held), rows, stop - start), jnp.bfloat16)
            for held, start, stop in parts
        ),
        in_specs=[pl.BlockSpec(memory_space=pltpu.SMEM)] * 3 + [whole] * (3 + len(arrived)),
        out_specs=(whole,) * len(parts),
        compiler_params=pltpu.CompilerParams(vmem_limit_bytes=8 * 2**20),
        cost_estimate=pl.CostEstimate(
            flops=tokens * width * width // 2, bytes_accessed=width * width, transcendentals=0
        ),
        name="share",
    )(*place, *[in_vmem(v) for v in (normed_t, grads, acc) + arrived])


def wide(value):
    return value.astype(jnp.float32)


def add_two_kernel(own, arrived, left, right):
    half = left.shape[2]
    total = wide(own[0]) + wide(arrived[0])
    left[0] = total[:, :half].astype(jnp.bfloat16)
    right[0] = total[:, half:].astype(jnp.bfloat16)


def add_side_kernel(own, arrived, from_before, from_after, after, before):
    half = from_before.shape[2]
    up, down = wide(own[1]) + wide(arrived[0]), wide(own[2]) + wide(arrived[1])
    after[0, :, :half] = (up[:, :half] + wide(from_before[0])).astype(jnp.bfloat16)
    after[0, :, half:] = up[:, half:].astype(jnp.bfloat16)
    before[0, :, :half] = down[:, :half].astype(jnp.bfloat16)
    before[0, :, half:] = (down[:, half:] + wide(from_after[0])).astype(jnp.bfloat16)


def add_both_kernel(near, far, near_before, near_after, far_before, far_after, after, before):
    half = near_before.shape[2]
    for which, (own, low, high) in enumerate(
        ((near, near_before, near_after), (far, far_before, far_after))
    ):
        after[which, :, :half] = (wide(own[0, :, :half]) + wide(low[0])).astype(jnp.bfloat16)
        after[which, :, half:] = own[0, :, half:]
        before[which, :, :half] = own[1, :, :half]
        before[which, :, half:] = (wide(own[1, :, half:]) + wide(high[0])).astype(jnp.bfloat16)


def add_far_kernel(own, from_before, from_after, out):
    out[0] = (wide(own[0]) + (wide(from_before[1]) + wide(from_after[1]))).astype(jnp.bfloat16)


def add_last_kernel(
    low_own,
    low_arrived,
    low_before,
    low_after,
    high_own,
    high_before,
    high_after,
    high_arrived,
    product,
    gain_sum,
):
    rows, width = product.shape
    low = (wide(low_own[3]) + wide(low_arrived[2])) + (wide(low_before[0]) + wide(low_after[0]))
    high = (wide(high_own[0]) + wide(high_arrived[0])) + (
        wide(high_before[0]) + wide(high_after[0])
    )
    for total, columns in ((low, slice(0, width // 2)), (high, slice(width // 2, width))):
        product[:, columns] = total[:rows].astype(jnp.bfloat16)
        gain_sum[:, columns] = jnp.sum(total[rows:], 0, keepdims=True)


def add_call(kernel, out_shape, name, *values):
    return pl.pallas_call(
        kernel,
        out_shape=out_shape,
        in_specs=[whole] * len(values),
        out_specs=(whole,) * len(out_shape),
        compiler_params=pltpu.CompilerParams(vmem_limit_bytes=8 * 2**20),
        name=name,
    )(*[in_vmem(v) for v in values])


def fsdp_move(value, dx=0, dy=0, dc=0):
    pairs = []
    for x in range(2):
        for y in range(ring):
            for c in range(2):
                target = ((x + dx) % 2 * ring + (y + dy) % ring) * 2 + (c + dc) % 2
                pairs.append(((x * ring + y) * 2 + c, target))
    return lax.ppermute(value, "fsdp", pairs)


turns = (2, 1, 3, 0)


def scatter_sum(place, normed_t, grads, acc, own_rows):
    width = normed_t.shape[0]
    half, quarter = width // 2, width // 4
    everything = ((turns, 0, width),)
    high_parts = (
        ((2,), half, half + quarter),
        ((2,), half + quarter, width),
        ((1, 3), half, width),
        ((0,), half, width),
    )
    local = (normed_t, grads, acc)
    far_arrived = fsdp_move(share(1, 1, everything, place, *local)[0], dc=1)
    near_arrived = fsdp_move(share(1, 0, everything, place, *local)[0], dc=1)
    far_two, far_rest, far_left, far_right, far_side, far_same = share(
        0,
        1,
        (((2,), 0, half), ((1, 3, 0), 0, half)) + high_parts,
        place,
        *local,
        far_arrived,
    )
    far_two = fsdp_move(far_two, dx=1)
    far_before, far_after = fsdp_move(far_left, dy=1), fsdp_move(far_right, dy=-1)
    far_rest = fsdp_move(far_rest, dx=1)
    low, near_left, near_right, near_side, near_same = share(
        0, 0, ((turns, 0, half),) + high_parts, place, *local, near_arrived
    )
    near_before, near_after = fsdp_move(near_left, dy=1), fsdp_move(near_right, dy=-1)

    def shaped(count, columns):
        return pltpu.VMEM((count, low.shape[1], columns), jnp.bfloat16)

    after, before = add_call(
        add_both_kernel,
        (shaped(2, half),) * 2,
        "add_both",
        near_side,
        far_side,
        near_before,
        near_after,
        far_before,
        far_after,
    )
    high_before, high_after = fsdp_move(after, dy=1), fsdp_move(before, dy=-1)
    left, right = add_call(add_two_kernel, (shaped(1, quarter),) * 2, "add_two", low, far_two)
    from_before, from_after = fsdp_move(left, dy=1), fsdp_move(right, dy=-1)
    after, before = add_call(
        add_side_kernel,
        (shaped(1, half),) * 2,
        "add_side",
        low,
        far_rest,
        from_before,
        from_after,
    )
    low_before, low_after = fsdp_move(after, dy=1), fsdp_move(before, dy=-1)
    (far_sum,) = add_call(
        add_far_kernel, (shaped(1, half),), "add_far", far_same, high_before, high_after
    )
    high_arrived = fsdp_move(far_sum, dx=1)
    return add_call(
        add_last_kernel,
        (
            jax.ShapeDtypeStruct((own_rows, width), jnp.bfloat16),
            jax.ShapeDtypeStruct((1, width), jnp.float32),
        ),
        "add_last",
        low,
        far_rest,
        low_before,
        low_after,
        near_same,
        high_before,
        high_after,
        high_arrived,
    )


def flip_kernel(block, out):
    half = out.shape[1]
    out[0] = block[:, :half].T
    out[1] = block[:, half:].T


def flip(block):
    return pl.pallas_call(
        flip_kernel,
        out_shape=jax.ShapeDtypeStruct(
            (2, block.shape[1] // 2, block.shape[0]), block.dtype
        ),
        in_specs=[whole],
        out_specs=whole,
        name="flip",
    )(block)


def gather_weight(block):
    own = flip(block)
    below, above = fsdp_move(own, dy=1), fsdp_move(own, dy=-1)
    beside = fsdp_move(own, dx=1)
    up = fsdp_move(jnp.stack([below[0], beside[0]]), dy=1)
    down = fsdp_move(jnp.stack([above[1], beside[1]]), dy=-1)
    mixed = fsdp_move(jnp.stack([below[1], above[0]]), dx=1)
    quarter = own.shape[1] // 2
    last_up = fsdp_move(up[1, :quarter], dy=1)
    last_down = fsdp_move(down[1, :quarter], dy=-1)
    last = fsdp_move(jnp.stack([up[0, quarter:], down[0, quarter:]]), dx=1)
    pieces = (own, below, above, beside, up, down, mixed, last, last_up, last_down)
    return pieces + tuple(fsdp_move(piece, dc=1) for piece in pieces)


sources = (
    (0, 0, ((0, 0), (0, 1))),
    (0, 3, ((1, 0), (1, 1))),
    (0, 1, ((2, 0), (2, 1))),
    (1, 0, ((3, 0), (3, 1))),
    (0, 2, ((4, 0), (5, 0))),
    (1, 3, ((4, 1), (6, 0))),
    (1, 1, ((6, 1), (5, 1))),
    (1, 2, ((8, None), (7, 0), (9, None), (7, 1))),
)


def top_kernel(at_x, at_y, at_core, *refs):
    received = refs[:20]
    head_in, both, pool_in, counts, labels, spread, weight, grads = refs[20:28]
    product, head, sems, head_sem = refs[28:]
    head_copy = pltpu.make_async_copy(head_in, head, head_sem)
    along_x, along_y, core = at_x[0], at_y[0], at_core[0]
    chips, copies = [], []
    for order, (dx, dy, stretches) in enumerate(sources):
        chip = (along_x ^ dx) * ring + lax.rem(along_y + dy, ring)
        chips.append(chip)
        size = weight.shape[1] // len(stretches)
        copies.append([])
        for dc in range(2):
            for part, (piece_index, which) in enumerate(stretches):
                piece = received[10 * dc + piece_index]
                copies[-1].append(
                    pltpu.make_async_copy(
                        piece if which is None else piece.at[which],
                        weight.at[2 * chip + (core ^ dc), part * size : (part + 1) * size, :],
                        sems.at[order, 4 * dc + part],
                    )
                )
        for copy in copies[-1]:
            copy.start()
    head_copy.start()
    for order, chip in enumerate(chips):
        for copy in copies[order]:
            copy.wait()
        part = lax.dot_general(
            jnp.concatenate([both[2 * chip], both[2 * chip + 1]], axis=1),
            jnp.concatenate([weight[2 * chip], weight[2 * chip + 1]], axis=1),
            (((1,), (1,)), ((), ())),
            preferred_element_type=jnp.float32,
        )
        product[...] = part if order == 0 else product[...] + part
    cands = counts.shape[0]
    y_pool = pool_in[...] + product[:cands, :] + product[cands:, :]
    pooled = (y_pool / counts[...]).astype(jnp.bfloat16)
    head_copy.wait()
    logits = jnp.dot(pooled, head[...], preferred_element_type=jnp.float32)
    classes = lax.broadcasted_iota(jnp.int32, logits.shape, 1)
    target = (labels[...] == classes).astype(jnp.float32)
    dlogit = (jax.nn.sigmoid(logits) - target).astype(jnp.bfloat16)
    dpool = lax.dot_general(
        dlogit, head[...], (((1,), (1,)), ((), ())), preferred_element_type=jnp.float32
    )
    cand_grad = (dpool / counts[...]).astype(jnp.bfloat16)
    grads[...] = jnp.dot(
        spread[...], cand_grad, preferred_element_type=jnp.float32
    ).astype(jnp.bfloat16)


def top_grads(place, layer_in, normed, gathered, head, segs, labels):
    batches, rows = segs.shape
    width = layer_in.shape[1]
    cands = labels.shape[1]
    onehot = (segs[:, None, :] == jnp.arange(cands, dtype=jnp.int32)[None, :, None]).astype(
        jnp.bfloat16
    )
    counts = jnp.sum(onehot.astype(jnp.float32), -1).reshape(-1, 1)
    owner = (segs + cands * jnp.arange(batches, dtype=jnp.int32)[:, None]).reshape(-1, 1)
    spread = (owner == jnp.arange(batches * cands, dtype=jnp.int32)[None]).astype(jnp.bfloat16)

    def pool(value):
        return jnp.einsum(
            "mcr,mrd->mcd",
            onehot,
            value.reshape(batches, rows, width),
            preferred_element_type=jnp.float32,
        ).reshape(-1, width)

    pooled_normed = pool(normed)
    high = lax.reduce_precision(pooled_normed, 8, 7)
    low = pooled_normed - high
    both = jnp.concatenate([high, low]).astype(jnp.bfloat16)
    devices = 4 * ring
    both = both.reshape(-1, devices, width // devices).transpose(1, 0, 2)
    return pl.pallas_call(
        top_kernel,
        out_shape=(
            pltpu.VMEM((devices, width, width // devices), jnp.bfloat16),
            pltpu.VMEM(layer_in.shape, jnp.bfloat16),
        ),
        in_specs=[pl.BlockSpec(memory_space=pltpu.SMEM)] * 3
        + [pl.BlockSpec(memory_space=pltpu.HBM)] * 21
        + [whole] * 5,
        out_specs=(whole, whole),
        scratch_shapes=[
            pltpu.VMEM((2 * batches * cands, width), jnp.float32),
            pltpu.VMEM(head.shape, head.dtype),
            pltpu.SemaphoreType.DMA((len(sources), 8)),
            pltpu.SemaphoreType.DMA,
        ],
        compiler_params=pltpu.CompilerParams(vmem_limit_bytes=16 * 2**20),
        cost_estimate=pl.CostEstimate(
            flops=4 * batches * cands * width * width,
            bytes_accessed=width * width * 2,
            transcendentals=0,
        ),
        name="top",
    )(
        *place,
        *[pltpu.with_memory_space_constraint(v, pltpu.HBM) for v in gathered],
        pltpu.with_memory_space_constraint(head, pltpu.HBM),
        both,
        pool(layer_in),
        counts,
        labels.reshape(-1, 1),
        spread,
    )


def per_device(acts, gains, proj, head, segs, labels):
    layer_in = acts[0]
    gain = gains[0]
    sections = lax.axis_size("section")
    section_pos = lax.axis_index("section")
    tokens, width = layer_in.shape
    gathered = gather_weight(proj[0])
    x_float = layer_in.astype(jnp.float32)
    inv_rms = lax.rsqrt(jnp.mean(x_float * x_float, -1, keepdims=True) + norm_eps)
    normed = (x_float * inv_rms * gain).astype(jnp.bfloat16)
    fsdp_pos = lax.axis_index("fsdp")
    place = tuple(
        jnp.reshape(value, (1,)).astype(jnp.int32)
        for value in (fsdp_pos // (2 * ring), fsdp_pos // 2 % ring, fsdp_pos % 2)
    )
    from_top = jnp.reshape(sections - 1 - section_pos, (1,)).astype(jnp.int32)
    weight, grads = top_grads(place, layer_in, normed, gathered, head, segs, labels)

    pieces = tokens // piece
    din = jnp.zeros((tokens, width), jnp.bfloat16)
    acc = jnp.zeros((extra, width), jnp.float32)
    received = {}
    blank = jnp.zeros((piece, width), jnp.bfloat16)
    for step in range(pieces + lag * (sections - 1)):
        out, grads, din, acc = chain_step(
            step,
            from_top,
            received.pop(step - lag, blank),
            weight,
            layer_in,
            inv_rms,
            gain[None],
            grads,
            din,
            acc,
        )
        pairs = [
            (s, s - 1)
            for s in range(1, sections)
            if any(
                0 <= near - lag * (sections - 1 - s) < pieces
                for near in range(step - step % merged, step - step % merged + merged)
            )
        ]
        if pairs:
            received[step] = lax.ppermute(out, "section", pairs)

    weight_part, gain_total = scatter_sum(place, normed.T, grads, acc, proj.shape[1])
    return (din[None], weight_part[None], gain_total)


def solution(mesh):
    return jax.shard_map(
        per_device,
        mesh=mesh,
        in_specs=(
            P("section", "fsdp", None),
            P("section", None),
            P("section", "fsdp", None),
            P(),
            P("fsdp", None),
            P("fsdp", None),
        ),
        out_specs=(P("section", "fsdp", None), P("section", "fsdp", None), P("section", None)),
        check_vma=False,
    )
```

```python
import functools

import jax
import jax.numpy as jnp
from jax import lax
from jax.experimental import pallas as pl
from jax.experimental.pallas import tpu as pltpu
from jax.sharding import PartitionSpec as P

norm_eps = 1e-06
piece = 48
lag = 2
merged = 4
ring = 4
extra = 16


def step_kernel(
    step,
    last,
    place,
    recv,
    weight,
    acts,
    rms,
    gain,
    grads_in,
    din_in,
    acc_in,
    out,
    grads,
    din,
    acc,
    back,
):
    rows, width = recv.shape
    index = step - lag * place[0]

    @pl.when((index >= 0) & (index <= last))
    def _():
        row = pl.multiple_of(index * rows, 16)
        here = pl.ds(row, rows)

        @pl.when(place[0] > 0)
        def _():
            grads[here, :] = recv[...]

        grad = grads[here, :]
        inv_rms = rms[here, :]
        partial = jnp.zeros((rows, 128), jnp.float32)
        for pair in range(width // 256):
            columns = slice(pair * 256, (pair + 1) * 256)
            block = jnp.dot(
                grad,
                jnp.concatenate([weight[2 * pair], weight[2 * pair + 1]], axis=1),
                preferred_element_type=jnp.float32,
            )
            back[:, columns] = block
            along = block * (acts[here, columns].astype(jnp.float32) * inv_rms)
            acc[:, columns] += jnp.sum(along.reshape(rows // extra, extra, 256), 0)
            along = along * gain[:, columns]
            partial = partial + along[:, :128] + along[:, 128:]
        mean = jnp.sum(partial, -1, keepdims=True) * (1.0 / width)
        x_hat = acts[here, :].astype(jnp.float32) * inv_rms
        layer_grad = (
            grad.astype(jnp.float32) + inv_rms * (back[...] * gain[...] - x_hat * mean)
        ).astype(jnp.bfloat16)
        out[...] = layer_grad
        din[here, :] = layer_grad


def in_vmem(value):
    return pltpu.with_memory_space_constraint(value, pltpu.VMEM)


whole = pl.BlockSpec(memory_space=pltpu.VMEM)


def chain_step(step, place, recv, weight, acts, rms, gain, grads, din, acc):
    rows, width = recv.shape
    return pl.pallas_call(
        functools.partial(step_kernel, step, acts.shape[0] // rows - 1),
        out_shape=(
            pltpu.VMEM((rows, width), jnp.bfloat16),
            pltpu.VMEM(grads.shape, grads.dtype),
            pltpu.VMEM(din.shape, din.dtype),
            pltpu.VMEM(acc.shape, acc.dtype),
        ),
        in_specs=[pl.BlockSpec(memory_space=pltpu.SMEM)] + [whole] * 8,
        out_specs=(whole,) * 4,
        input_output_aliases={6: 1, 7: 2, 8: 3},
        scratch_shapes=[pltpu.VMEM((rows, width), jnp.float32)],
        compiler_params=pltpu.CompilerParams(vmem_limit_bytes=8 * 2**20),
        cost_estimate=pl.CostEstimate(
            flops=2 * rows * width * width, bytes_accessed=width * width * 2, transcendentals=0
        ),
        name="chain_step",
    )(place, *[in_vmem(v) for v in (recv, weight, acts, rms, gain, grads, din, acc)])


def share_kernel(other, across, parts, at_x, at_y, at_core, normed_t, grads, acc, *rest):
    outs = rest[len(rest) - len(parts) :]
    arrived = rest[: len(rest) - len(parts)]
    rows = outs[0].shape[1] - extra
    along_x, along_y, core = at_x[0], at_y[0], at_core[0]
    for slot, turn in enumerate(turns):
        block = (
            (along_x ^ across) * (2 * ring) + lax.rem(along_y + turn, ring) * 2 + (core ^ other)
        )
        value = jnp.dot(
            normed_t[pl.ds(pl.multiple_of(block * rows, rows), rows), :],
            grads[...],
            preferred_element_type=jnp.float32,
        )
        gain_rows = acc[...]
        if arrived:
            value = value + arrived[0][slot, :rows, :].astype(jnp.float32)
            gain_rows = gain_rows + arrived[0][slot, rows:, :].astype(jnp.float32)
        value = value.astype(jnp.bfloat16)
        gain_rows = gain_rows.astype(jnp.bfloat16)
        for out, (held, start, stop) in zip(outs, parts):
            if turn in held:
                out[held.index(turn), :rows, :] = value[:, start:stop]
                out[held.index(turn), rows:, :] = gain_rows[:, start:stop]


def share(other, across, parts, place, normed_t, grads, acc, *arrived):
    width, tokens = normed_t.shape
    rows = width // (4 * ring) + extra
    return pl.pallas_call(
        functools.partial(share_kernel, other, across, parts),
        out_shape=tuple(
            pltpu.VMEM((len(held), rows, stop - start), jnp.bfloat16)
            for held, start, stop in parts
        ),
        in_specs=[pl.BlockSpec(memory_space=pltpu.SMEM)] * 3 + [whole] * (3 + len(arrived)),
        out_specs=(whole,) * len(parts),
        compiler_params=pltpu.CompilerParams(vmem_limit_bytes=8 * 2**20),
        cost_estimate=pl.CostEstimate(
            flops=tokens * width * width // 2, bytes_accessed=width * width, transcendentals=0
        ),
        name="share",
    )(*place, *[in_vmem(v) for v in (normed_t, grads, acc) + arrived])


def wide(value):
    return value.astype(jnp.float32)


def add_two_kernel(own, arrived, left, right):
    half = left.shape[2]
    total = wide(own[0]) + wide(arrived[0])
    left[0] = total[:, :half].astype(jnp.bfloat16)
    right[0] = total[:, half:].astype(jnp.bfloat16)


def add_side_kernel(own, arrived, from_before, from_after, after, before):
    half = from_before.shape[2]
    up, down = wide(own[1]) + wide(arrived[1]), wide(own[2]) + wide(arrived[2])
    after[0, :, :half] = (up[:, :half] + wide(from_before[0])).astype(jnp.bfloat16)
    after[0, :, half:] = up[:, half:].astype(jnp.bfloat16)
    before[0, :, :half] = down[:, :half].astype(jnp.bfloat16)
    before[0, :, half:] = (down[:, half:] + wide(from_after[0])).astype(jnp.bfloat16)


def add_both_kernel(near, far, near_before, near_after, far_before, far_after, after, before):
    half = near_before.shape[2]
    for which, (own, low, high) in enumerate(
        ((near, near_before, near_after), (far, far_before, far_after))
    ):
        after[which, :, :half] = (wide(own[0, :, :half]) + wide(low[0])).astype(jnp.bfloat16)
        after[which, :, half:] = own[0, :, half:]
        before[which, :, :half] = own[1, :, :half]
        before[which, :, half:] = (wide(own[1, :, half:]) + wide(high[0])).astype(jnp.bfloat16)


def add_far_kernel(own, from_before, from_after, out):
    out[0] = (wide(own[0]) + (wide(from_before[1]) + wide(from_after[1]))).astype(jnp.bfloat16)


def add_last_kernel(
    low_own,
    low_arrived,
    low_before,
    low_after,
    high_own,
    high_before,
    high_after,
    high_arrived,
    product,
    gain_sum,
):
    rows, width = product.shape
    low = (wide(low_own[3]) + wide(low_arrived[3])) + (wide(low_before[0]) + wide(low_after[0]))
    high = (wide(high_own[0]) + wide(high_arrived[0])) + (
        wide(high_before[0]) + wide(high_after[0])
    )
    for total, columns in ((low, slice(0, width // 2)), (high, slice(width // 2, width))):
        product[:, columns] = total[:rows].astype(jnp.bfloat16)
        gain_sum[:, columns] = jnp.sum(total[rows:], 0, keepdims=True)


def add_call(kernel, out_shape, name, *values):
    return pl.pallas_call(
        kernel,
        out_shape=out_shape,
        in_specs=[whole] * len(values),
        out_specs=(whole,) * len(out_shape),
        compiler_params=pltpu.CompilerParams(vmem_limit_bytes=8 * 2**20),
        name=name,
    )(*[in_vmem(v) for v in values])


def fsdp_move(value, dx=0, dy=0, dc=0):
    pairs = []
    for x in range(2):
        for y in range(ring):
            for c in range(2):
                target = ((x + dx) % 2 * ring + (y + dy) % ring) * 2 + (c + dc) % 2
                pairs.append(((x * ring + y) * 2 + c, target))
    return lax.ppermute(value, "fsdp", pairs)


turns = (2, 1, 3, 0)


def scatter_sum(place, normed_t, grads, acc, own_rows):
    width = normed_t.shape[0]
    half, quarter = width // 2, width // 4
    everything = ((turns, 0, width),)
    high_parts = (
        ((2,), half, half + quarter),
        ((2,), half + quarter, width),
        ((1, 3), half, width),
        ((0,), half, width),
    )
    local = (normed_t, grads, acc)
    far_arrived = fsdp_move(share(1, 1, everything, place, *local)[0], dc=1)
    near_arrived = fsdp_move(share(1, 0, everything, place, *local)[0], dc=1)
    far_low, far_left, far_right, far_side, far_same = share(
        0,
        1,
        ((turns, 0, half),) + high_parts,
        place,
        *local,
        far_arrived,
    )
    far_low = fsdp_move(far_low, dx=1)
    far_before, far_after = fsdp_move(far_left, dy=1), fsdp_move(far_right, dy=-1)
    low, near_left, near_right, near_side, near_same = share(
        0, 0, ((turns, 0, half),) + high_parts, place, *local, near_arrived
    )
    near_before, near_after = fsdp_move(near_left, dy=1), fsdp_move(near_right, dy=-1)

    def shaped(count, columns):
        return pltpu.VMEM((count, low.shape[1], columns), jnp.bfloat16)

    after, before = add_call(
        add_both_kernel,
        (shaped(2, half),) * 2,
        "add_both",
        near_side,
        far_side,
        near_before,
        near_after,
        far_before,
        far_after,
    )
    high_before, high_after = fsdp_move(after, dy=1), fsdp_move(before, dy=-1)
    left, right = add_call(add_two_kernel, (shaped(1, quarter),) * 2, "add_two", low, far_low)
    from_before, from_after = fsdp_move(left, dy=1), fsdp_move(right, dy=-1)
    after, before = add_call(
        add_side_kernel,
        (shaped(1, half),) * 2,
        "add_side",
        low,
        far_low,
        from_before,
        from_after,
    )
    low_before, low_after = fsdp_move(after, dy=1), fsdp_move(before, dy=-1)
    (far_sum,) = add_call(
        add_far_kernel, (shaped(1, half),), "add_far", far_same, high_before, high_after
    )
    high_arrived = fsdp_move(far_sum, dx=1)
    return add_call(
        add_last_kernel,
        (
            jax.ShapeDtypeStruct((own_rows, width), jnp.bfloat16),
            jax.ShapeDtypeStruct((1, width), jnp.float32),
        ),
        "add_last",
        low,
        far_low,
        low_before,
        low_after,
        near_same,
        high_before,
        high_after,
        high_arrived,
    )


def flip_kernel(block, out):
    half = out.shape[1]
    out[0] = block[:, :half].T
    out[1] = block[:, half:].T


def flip(block):
    return pl.pallas_call(
        flip_kernel,
        out_shape=jax.ShapeDtypeStruct(
            (2, block.shape[1] // 2, block.shape[0]), block.dtype
        ),
        in_specs=[whole],
        out_specs=whole,
        name="flip",
    )(block)


def gather_weight(block):
    own = flip(block)
    below, above = fsdp_move(own, dy=1), fsdp_move(own, dy=-1)
    beside = fsdp_move(own, dx=1)
    up = fsdp_move(jnp.stack([below[0], beside[0]]), dy=1)
    down = fsdp_move(jnp.stack([above[1], beside[1]]), dy=-1)
    mixed = fsdp_move(jnp.stack([below[1], above[0]]), dx=1)
    quarter = own.shape[1] // 2
    last_up = fsdp_move(up[1, :quarter], dy=1)
    last_down = fsdp_move(down[1, :quarter], dy=-1)
    last = fsdp_move(jnp.stack([up[0, quarter:], down[0, quarter:]]), dx=1)
    pieces = (own, below, above, beside, up, down, mixed, last, last_up, last_down)
    return pieces + tuple(fsdp_move(piece, dc=1) for piece in pieces)


sources = (
    (0, 0, ((0, 0), (0, 1))),
    (0, 3, ((1, 0), (1, 1))),
    (0, 1, ((2, 0), (2, 1))),
    (1, 0, ((3, 0), (3, 1))),
    (0, 2, ((4, 0), (5, 0))),
    (1, 3, ((4, 1), (6, 0))),
    (1, 1, ((6, 1), (5, 1))),
    (1, 2, ((8, None), (7, 0), (9, None), (7, 1))),
)


def top_kernel(at_x, at_y, at_core, *refs):
    received = refs[:20]
    head_in, both, pool_in, counts, labels, spread, weight, grads = refs[20:28]
    product, head, sems, head_sem = refs[28:]
    head_copy = pltpu.make_async_copy(head_in, head, head_sem)
    along_x, along_y, core = at_x[0], at_y[0], at_core[0]
    chips, copies = [], []
    for order, (dx, dy, stretches) in enumerate(sources):
        chip = (along_x ^ dx) * ring + lax.rem(along_y + dy, ring)
        chips.append(chip)
        size = weight.shape[1] // len(stretches)
        copies.append([])
        for dc in range(2):
            for part, (piece_index, which) in enumerate(stretches):
                piece = received[10 * dc + piece_index]
                copies[-1].append(
                    pltpu.make_async_copy(
                        piece if which is None else piece.at[which],
                        weight.at[2 * chip + (core ^ dc), part * size : (part + 1) * size, :],
                        sems.at[order, 4 * dc + part],
                    )
                )
        for copy in copies[-1]:
            copy.start()
    head_copy.start()
    for order, chip in enumerate(chips):
        for copy in copies[order]:
            copy.wait()
        part = lax.dot_general(
            jnp.concatenate([both[2 * chip], both[2 * chip + 1]], axis=1),
            jnp.concatenate([weight[2 * chip], weight[2 * chip + 1]], axis=1),
            (((1,), (1,)), ((), ())),
            preferred_element_type=jnp.float32,
        )
        product[...] = part if order == 0 else product[...] + part
    cands = counts.shape[0]
    y_pool = pool_in[...] + product[:cands, :] + product[cands:, :]
    pooled = (y_pool / counts[...]).astype(jnp.bfloat16)
    head_copy.wait()
    logits = jnp.dot(pooled, head[...], preferred_element_type=jnp.float32)
    classes = lax.broadcasted_iota(jnp.int32, logits.shape, 1)
    target = (labels[...] == classes).astype(jnp.float32)
    dlogit = (jax.nn.sigmoid(logits) - target).astype(jnp.bfloat16)
    dpool = lax.dot_general(
        dlogit, head[...], (((1,), (1,)), ((), ())), preferred_element_type=jnp.float32
    )
    cand_grad = (dpool / counts[...]).astype(jnp.bfloat16)
    grads[...] = jnp.dot(
        spread[...], cand_grad, preferred_element_type=jnp.float32
    ).astype(jnp.bfloat16)


def top_grads(place, layer_in, normed, gathered, head, segs, labels):
    batches, rows = segs.shape
    width = layer_in.shape[1]
    cands = labels.shape[1]
    onehot = (segs[:, None, :] == jnp.arange(cands, dtype=jnp.int32)[None, :, None]).astype(
        jnp.bfloat16
    )
    counts = jnp.sum(onehot.astype(jnp.float32), -1).reshape(-1, 1)
    owner = (segs + cands * jnp.arange(batches, dtype=jnp.int32)[:, None]).reshape(-1, 1)
    spread = (owner == jnp.arange(batches * cands, dtype=jnp.int32)[None]).astype(jnp.bfloat16)

    def pool(value):
        return jnp.einsum(
            "mcr,mrd->mcd",
            onehot,
            value.reshape(batches, rows, width),
            preferred_element_type=jnp.float32,
        ).reshape(-1, width)

    pooled_normed = pool(normed)
    high = lax.reduce_precision(pooled_normed, 8, 7)
    low = pooled_normed - high
    both = jnp.concatenate([high, low]).astype(jnp.bfloat16)
    devices = 4 * ring
    both = both.reshape(-1, devices, width // devices).transpose(1, 0, 2)
    return pl.pallas_call(
        top_kernel,
        out_shape=(
            pltpu.VMEM((devices, width, width // devices), jnp.bfloat16),
            pltpu.VMEM(layer_in.shape, jnp.bfloat16),
        ),
        in_specs=[pl.BlockSpec(memory_space=pltpu.SMEM)] * 3
        + [pl.BlockSpec(memory_space=pltpu.HBM)] * 21
        + [whole] * 5,
        out_specs=(whole, whole),
        scratch_shapes=[
            pltpu.VMEM((2 * batches * cands, width), jnp.float32),
            pltpu.VMEM(head.shape, head.dtype),
            pltpu.SemaphoreType.DMA((len(sources), 8)),
            pltpu.SemaphoreType.DMA,
        ],
        compiler_params=pltpu.CompilerParams(vmem_limit_bytes=16 * 2**20),
        cost_estimate=pl.CostEstimate(
            flops=4 * batches * cands * width * width,
            bytes_accessed=width * width * 2,
            transcendentals=0,
        ),
        name="top",
    )(
        *place,
        *[pltpu.with_memory_space_constraint(v, pltpu.HBM) for v in gathered],
        pltpu.with_memory_space_constraint(head, pltpu.HBM),
        both,
        pool(layer_in),
        counts,
        labels.reshape(-1, 1),
        spread,
    )


def per_device(acts, gains, proj, head, segs, labels):
    layer_in = acts[0]
    gain = gains[0]
    sections = lax.axis_size("section")
    section_pos = lax.axis_index("section")
    tokens, width = layer_in.shape
    gathered = gather_weight(proj[0])
    x_float = layer_in.astype(jnp.float32)
    inv_rms = lax.rsqrt(jnp.mean(x_float * x_float, -1, keepdims=True) + norm_eps)
    normed = (x_float * inv_rms * gain).astype(jnp.bfloat16)
    fsdp_pos = lax.axis_index("fsdp")
    place = tuple(
        jnp.reshape(value, (1,)).astype(jnp.int32)
        for value in (fsdp_pos // (2 * ring), fsdp_pos // 2 % ring, fsdp_pos % 2)
    )
    from_top = jnp.reshape(sections - 1 - section_pos, (1,)).astype(jnp.int32)
    weight, grads = top_grads(place, layer_in, normed, gathered, head, segs, labels)

    pieces = tokens // piece
    din = jnp.zeros((tokens, width), jnp.bfloat16)
    acc = jnp.zeros((extra, width), jnp.float32)
    received = {}
    blank = jnp.zeros((piece, width), jnp.bfloat16)
    for step in range(pieces + lag * (sections - 1)):
        out, grads, din, acc = chain_step(
            step,
            from_top,
            received.pop(step - lag, blank),
            weight,
            layer_in,
            inv_rms,
            gain[None],
            grads,
            din,
            acc,
        )
        pairs = [
            (s, s - 1)
            for s in range(1, sections)
            if any(
                0 <= near - lag * (sections - 1 - s) < pieces
                for near in range(step - step % merged, step - step % merged + merged)
            )
        ]
        if pairs:
            received[step] = lax.ppermute(out, "section", pairs)

    weight_part, gain_total = scatter_sum(place, normed.T, grads, acc, proj.shape[1])
    return (din[None], weight_part[None], gain_total)


def solution(mesh):
    return jax.shard_map(
        per_device,
        mesh=mesh,
        in_specs=(
            P("section", "fsdp", None),
            P("section", None),
            P("section", "fsdp", None),
            P(),
            P("fsdp", None),
            P("fsdp", None),
        ),
        out_specs=(P("section", "fsdp", None), P("section", "fsdp", None), P("section", None)),
        check_vma=False,
    )
```

```python
import functools

import jax
import jax.numpy as jnp
from jax import lax
from jax.experimental import pallas as pl
from jax.experimental.pallas import tpu as pltpu
from jax.sharding import PartitionSpec as P

norm_eps = 1e-06
piece = 48
lag = 3
merged = 7
ring = 4
extra = 16


def step_kernel(
    step,
    last,
    place,
    recv,
    weight,
    acts,
    rms,
    gain,
    grads_in,
    din_in,
    acc_in,
    out,
    grads,
    din,
    acc,
    back,
):
    rows, width = recv.shape
    index = step - lag * place[0]

    @pl.when((index >= 0) & (index <= last))
    def _():
        row = pl.multiple_of(index * rows, 16)
        here = pl.ds(row, rows)

        @pl.when(place[0] > 0)
        def _():
            grads[here, :] = recv[...]

        grad = grads[here, :]
        inv_rms = rms[here, :]
        partial = jnp.zeros((rows, 128), jnp.float32)
        for pair in range(width // 256):
            columns = slice(pair * 256, (pair + 1) * 256)
            block = jnp.dot(
                grad,
                jnp.concatenate([weight[2 * pair], weight[2 * pair + 1]], axis=1),
                preferred_element_type=jnp.float32,
            )
            back[:, columns] = block
            along = block * (acts[here, columns].astype(jnp.float32) * inv_rms)
            acc[:, columns] += jnp.sum(along.reshape(rows // extra, extra, 256), 0)
            along = along * gain[:, columns]
            partial = partial + along[:, :128] + along[:, 128:]
        mean = jnp.sum(partial, -1, keepdims=True) * (1.0 / width)
        x_hat = acts[here, :].astype(jnp.float32) * inv_rms
        layer_grad = (
            grad.astype(jnp.float32) + inv_rms * (back[...] * gain[...] - x_hat * mean)
        ).astype(jnp.bfloat16)
        out[...] = layer_grad
        din[here, :] = layer_grad


def in_vmem(value):
    return pltpu.with_memory_space_constraint(value, pltpu.VMEM)


whole = pl.BlockSpec(memory_space=pltpu.VMEM)


def chain_step(step, place, recv, weight, acts, rms, gain, grads, din, acc):
    rows, width = recv.shape
    return pl.pallas_call(
        functools.partial(step_kernel, step, acts.shape[0] // rows - 1),
        out_shape=(
            pltpu.VMEM((rows, width), jnp.bfloat16),
            pltpu.VMEM(grads.shape, grads.dtype),
            pltpu.VMEM(din.shape, din.dtype),
            pltpu.VMEM(acc.shape, acc.dtype),
        ),
        in_specs=[pl.BlockSpec(memory_space=pltpu.SMEM)] + [whole] * 8,
        out_specs=(whole,) * 4,
        input_output_aliases={6: 1, 7: 2, 8: 3},
        scratch_shapes=[pltpu.VMEM((rows, width), jnp.float32)],
        compiler_params=pltpu.CompilerParams(vmem_limit_bytes=8 * 2**20),
        cost_estimate=pl.CostEstimate(
            flops=2 * rows * width * width, bytes_accessed=width * width * 2, transcendentals=0
        ),
        name="chain_step",
    )(place, *[in_vmem(v) for v in (recv, weight, acts, rms, gain, grads, din, acc)])


def share_kernel(other, across, parts, at_x, at_y, at_core, normed_t, grads, acc, *rest):
    outs = rest[len(rest) - len(parts) :]
    arrived = rest[: len(rest) - len(parts)]
    rows = outs[0].shape[1] - extra
    along_x, along_y, core = at_x[0], at_y[0], at_core[0]
    for slot, turn in enumerate(turns):
        block = (
            (along_x ^ across) * (2 * ring) + lax.rem(along_y + turn, ring) * 2 + (core ^ other)
        )
        value = jnp.dot(
            normed_t[pl.ds(pl.multiple_of(block * rows, rows), rows), :],
            grads[...],
            preferred_element_type=jnp.float32,
        )
        gain_rows = acc[...]
        if arrived:
            value = value + arrived[0][slot, :rows, :].astype(jnp.float32)
            gain_rows = gain_rows + arrived[0][slot, rows:, :].astype(jnp.float32)
        value = value.astype(jnp.bfloat16)
        gain_rows = gain_rows.astype(jnp.bfloat16)
        for out, (held, start, stop) in zip(outs, parts):
            if turn in held:
                out[held.index(turn), :rows, :] = value[:, start:stop]
                out[held.index(turn), rows:, :] = gain_rows[:, start:stop]


def share(other, across, parts, place, normed_t, grads, acc, *arrived):
    width, tokens = normed_t.shape
    rows = width // (4 * ring) + extra
    return pl.pallas_call(
        functools.partial(share_kernel, other, across, parts),
        out_shape=tuple(
            pltpu.VMEM((len(held), rows, stop - start), jnp.bfloat16)
            for held, start, stop in parts
        ),
        in_specs=[pl.BlockSpec(memory_space=pltpu.SMEM)] * 3 + [whole] * (3 + len(arrived)),
        out_specs=(whole,) * len(parts),
        compiler_params=pltpu.CompilerParams(vmem_limit_bytes=8 * 2**20),
        cost_estimate=pl.CostEstimate(
            flops=tokens * width * width // 2, bytes_accessed=width * width, transcendentals=0
        ),
        name="share",
    )(*place, *[in_vmem(v) for v in (normed_t, grads, acc) + arrived])


def wide(value):
    return value.astype(jnp.float32)


def add_two_kernel(own, arrived, left, right):
    half = left.shape[2]
    total = wide(own[0]) + wide(arrived[0])
    left[0] = total[:, :half].astype(jnp.bfloat16)
    right[0] = total[:, half:].astype(jnp.bfloat16)


def add_side_kernel(own, arrived, from_before, from_after, after, before):
    half = from_before.shape[2]
    up, down = wide(own[1]) + wide(arrived[1]), wide(own[2]) + wide(arrived[2])
    after[0, :, :half] = (up[:, :half] + wide(from_before[0])).astype(jnp.bfloat16)
    after[0, :, half:] = up[:, half:].astype(jnp.bfloat16)
    before[0, :, :half] = down[:, :half].astype(jnp.bfloat16)
    before[0, :, half:] = (down[:, half:] + wide(from_after[0])).astype(jnp.bfloat16)


def add_both_kernel(near, far, near_before, near_after, far_before, far_after, after, before):
    half = near_before.shape[2]
    for which, (own, low, high) in enumerate(
        ((near, near_before, near_after), (far, far_before, far_after))
    ):
        after[which, :, :half] = (wide(own[0, :, :half]) + wide(low[0])).astype(jnp.bfloat16)
        after[which, :, half:] = own[0, :, half:]
        before[which, :, :half] = own[1, :, :half]
        before[which, :, half:] = (wide(own[1, :, half:]) + wide(high[0])).astype(jnp.bfloat16)


def add_far_kernel(own, from_before, from_after, out):
    out[0] = (wide(own[0]) + (wide(from_before[1]) + wide(from_after[1]))).astype(jnp.bfloat16)


def add_last_kernel(
    low_own,
    low_arrived,
    low_before,
    low_after,
    high_own,
    high_before,
    high_after,
    high_arrived,
    product,
    gain_sum,
):
    rows, width = product.shape
    low = (wide(low_own[3]) + wide(low_arrived[3])) + (wide(low_before[0]) + wide(low_after[0]))
    high = (wide(high_own[0]) + wide(high_arrived[0])) + (
        wide(high_before[0]) + wide(high_after[0])
    )
    for total, columns in ((low, slice(0, width // 2)), (high, slice(width // 2, width))):
        product[:, columns] = total[:rows].astype(jnp.bfloat16)
        gain_sum[:, columns] = jnp.sum(total[rows:], 0, keepdims=True)


def add_call(kernel, out_shape, name, *values):
    return pl.pallas_call(
        kernel,
        out_shape=out_shape,
        in_specs=[whole] * len(values),
        out_specs=(whole,) * len(out_shape),
        compiler_params=pltpu.CompilerParams(vmem_limit_bytes=8 * 2**20),
        name=name,
    )(*[in_vmem(v) for v in values])


def fsdp_move(value, dx=0, dy=0, dc=0):
    pairs = []
    for x in range(2):
        for y in range(ring):
            for c in range(2):
                target = ((x + dx) % 2 * ring + (y + dy) % ring) * 2 + (c + dc) % 2
                pairs.append(((x * ring + y) * 2 + c, target))
    return lax.ppermute(value, "fsdp", pairs)


turns = (2, 1, 3, 0)


def scatter_sum(place, normed_t, grads, acc, own_rows):
    width = normed_t.shape[0]
    half, quarter = width // 2, width // 4
    everything = ((turns, 0, width),)
    high_parts = (
        ((2,), half, half + quarter),
        ((2,), half + quarter, width),
        ((1, 3), half, width),
        ((0,), half, width),
    )
    local = (normed_t, grads, acc)
    far_arrived = fsdp_move(share(1, 1, everything, place, *local)[0], dc=1)
    near_arrived = fsdp_move(share(1, 0, everything, place, *local)[0], dc=1)
    far_low, far_left, far_right, far_side, far_same = share(
        0,
        1,
        ((turns, 0, half),) + high_parts,
        place,
        *local,
        far_arrived,
    )
    far_low = fsdp_move(far_low, dx=1)
    far_before, far_after = fsdp_move(far_left, dy=1), fsdp_move(far_right, dy=-1)
    low, near_left, near_right, near_side, near_same = share(
        0, 0, ((turns, 0, half),) + high_parts, place, *local, near_arrived
    )
    near_before, near_after = fsdp_move(near_left, dy=1), fsdp_move(near_right, dy=-1)

    def shaped(count, columns):
        return pltpu.VMEM((count, low.shape[1], columns), jnp.bfloat16)

    after, before = add_call(
        add_both_kernel,
        (shaped(2, half),) * 2,
        "add_both",
        near_side,
        far_side,
        near_before,
        near_after,
        far_before,
        far_after,
    )
    high_before, high_after = fsdp_move(after, dy=1), fsdp_move(before, dy=-1)
    left, right = add_call(add_two_kernel, (shaped(1, quarter),) * 2, "add_two", low, far_low)
    from_before, from_after = fsdp_move(left, dy=1), fsdp_move(right, dy=-1)
    after, before = add_call(
        add_side_kernel,
        (shaped(1, half),) * 2,
        "add_side",
        low,
        far_low,
        from_before,
        from_after,
    )
    low_before, low_after = fsdp_move(after, dy=1), fsdp_move(before, dy=-1)
    (far_sum,) = add_call(
        add_far_kernel, (shaped(1, half),), "add_far", far_same, high_before, high_after
    )
    high_arrived = fsdp_move(far_sum, dx=1)
    return add_call(
        add_last_kernel,
        (
            jax.ShapeDtypeStruct((own_rows, width), jnp.bfloat16),
            jax.ShapeDtypeStruct((1, width), jnp.float32),
        ),
        "add_last",
        low,
        far_low,
        low_before,
        low_after,
        near_same,
        high_before,
        high_after,
        high_arrived,
    )


def flip_kernel(block, out):
    half = out.shape[1]
    out[0] = block[:, :half].T
    out[1] = block[:, half:].T


def flip(block):
    return pl.pallas_call(
        flip_kernel,
        out_shape=jax.ShapeDtypeStruct(
            (2, block.shape[1] // 2, block.shape[0]), block.dtype
        ),
        in_specs=[whole],
        out_specs=whole,
        name="flip",
    )(block)


def gather_weight(block):
    own = flip(block)
    below, above = fsdp_move(own, dy=1), fsdp_move(own, dy=-1)
    beside = fsdp_move(own, dx=1)
    up = fsdp_move(jnp.stack([below[0], beside[0]]), dy=1)
    down = fsdp_move(jnp.stack([above[1], beside[1]]), dy=-1)
    mixed = fsdp_move(jnp.stack([below[1], above[0]]), dx=1)
    quarter = own.shape[1] // 2
    last_up = fsdp_move(up[1, :quarter], dy=1)
    last_down = fsdp_move(down[1, :quarter], dy=-1)
    last = fsdp_move(jnp.stack([up[0, quarter:], down[0, quarter:]]), dx=1)
    pieces = (own, below, above, beside, up, down, mixed, last, last_up, last_down)
    return pieces + tuple(fsdp_move(piece, dc=1) for piece in pieces)


sources = (
    (0, 0, ((0, 0), (0, 1))),
    (0, 3, ((1, 0), (1, 1))),
    (0, 1, ((2, 0), (2, 1))),
    (1, 0, ((3, 0), (3, 1))),
    (0, 2, ((4, 0), (5, 0))),
    (1, 3, ((4, 1), (6, 0))),
    (1, 1, ((6, 1), (5, 1))),
    (1, 2, ((8, None), (7, 0), (9, None), (7, 1))),
)


def top_kernel(at_x, at_y, at_core, *refs):
    received = refs[:20]
    head_in, both, pool_in, counts, labels, spread, weight, grads = refs[20:28]
    product, head, sems, head_sem = refs[28:]
    head_copy = pltpu.make_async_copy(head_in, head, head_sem)
    along_x, along_y, core = at_x[0], at_y[0], at_core[0]
    chips, copies = [], []
    for order, (dx, dy, stretches) in enumerate(sources):
        chip = (along_x ^ dx) * ring + lax.rem(along_y + dy, ring)
        chips.append(chip)
        size = weight.shape[1] // len(stretches)
        copies.append([])
        for dc in range(2):
            for part, (piece_index, which) in enumerate(stretches):
                piece = received[10 * dc + piece_index]
                copies[-1].append(
                    pltpu.make_async_copy(
                        piece if which is None else piece.at[which],
                        weight.at[2 * chip + (core ^ dc), part * size : (part + 1) * size, :],
                        sems.at[order, 4 * dc + part],
                    )
                )
        for copy in copies[-1]:
            copy.start()
    head_copy.start()
    for order, chip in enumerate(chips):
        for copy in copies[order]:
            copy.wait()
        part = lax.dot_general(
            jnp.concatenate([both[2 * chip], both[2 * chip + 1]], axis=1),
            jnp.concatenate([weight[2 * chip], weight[2 * chip + 1]], axis=1),
            (((1,), (1,)), ((), ())),
            preferred_element_type=jnp.float32,
        )
        product[...] = part if order == 0 else product[...] + part
    cands = counts.shape[0]
    y_pool = pool_in[...] + product[:cands, :] + product[cands:, :]
    pooled = (y_pool / counts[...]).astype(jnp.bfloat16)
    head_copy.wait()
    logits = jnp.dot(pooled, head[...], preferred_element_type=jnp.float32)
    classes = lax.broadcasted_iota(jnp.int32, logits.shape, 1)
    target = (labels[...] == classes).astype(jnp.float32)
    dlogit = (jax.nn.sigmoid(logits) - target).astype(jnp.bfloat16)
    dpool = lax.dot_general(
        dlogit, head[...], (((1,), (1,)), ((), ())), preferred_element_type=jnp.float32
    )
    cand_grad = (dpool / counts[...]).astype(jnp.bfloat16)
    grads[...] = jnp.dot(
        spread[...], cand_grad, preferred_element_type=jnp.float32
    ).astype(jnp.bfloat16)


def top_grads(place, layer_in, normed, gathered, head, segs, labels):
    batches, rows = segs.shape
    width = layer_in.shape[1]
    cands = labels.shape[1]
    onehot = (segs[:, None, :] == jnp.arange(cands, dtype=jnp.int32)[None, :, None]).astype(
        jnp.bfloat16
    )
    counts = jnp.sum(onehot.astype(jnp.float32), -1).reshape(-1, 1)
    owner = (segs + cands * jnp.arange(batches, dtype=jnp.int32)[:, None]).reshape(-1, 1)
    spread = (owner == jnp.arange(batches * cands, dtype=jnp.int32)[None]).astype(jnp.bfloat16)

    def pool(value):
        return jnp.einsum(
            "mcr,mrd->mcd",
            onehot,
            value.reshape(batches, rows, width),
            preferred_element_type=jnp.float32,
        ).reshape(-1, width)

    pooled_normed = pool(normed)
    high = lax.reduce_precision(pooled_normed, 8, 7)
    low = pooled_normed - high
    both = jnp.concatenate([high, low]).astype(jnp.bfloat16)
    devices = 4 * ring
    both = both.reshape(-1, devices, width // devices).transpose(1, 0, 2)
    return pl.pallas_call(
        top_kernel,
        out_shape=(
            pltpu.VMEM((devices, width, width // devices), jnp.bfloat16),
            pltpu.VMEM(layer_in.shape, jnp.bfloat16),
        ),
        in_specs=[pl.BlockSpec(memory_space=pltpu.SMEM)] * 3
        + [pl.BlockSpec(memory_space=pltpu.HBM)] * 21
        + [whole] * 5,
        out_specs=(whole, whole),
        scratch_shapes=[
            pltpu.VMEM((2 * batches * cands, width), jnp.float32),
            pltpu.VMEM(head.shape, head.dtype),
            pltpu.SemaphoreType.DMA((len(sources), 8)),
            pltpu.SemaphoreType.DMA,
        ],
        compiler_params=pltpu.CompilerParams(vmem_limit_bytes=16 * 2**20),
        cost_estimate=pl.CostEstimate(
            flops=4 * batches * cands * width * width,
            bytes_accessed=width * width * 2,
            transcendentals=0,
        ),
        name="top",
    )(
        *place,
        *[pltpu.with_memory_space_constraint(v, pltpu.HBM) for v in gathered],
        pltpu.with_memory_space_constraint(head, pltpu.HBM),
        both,
        pool(layer_in),
        counts,
        labels.reshape(-1, 1),
        spread,
    )


def per_device(acts, gains, proj, head, segs, labels):
    layer_in = acts[0]
    gain = gains[0]
    sections = lax.axis_size("section")
    section_pos = lax.axis_index("section")
    tokens, width = layer_in.shape
    gathered = gather_weight(proj[0])
    x_float = layer_in.astype(jnp.float32)
    inv_rms = lax.rsqrt(jnp.mean(x_float * x_float, -1, keepdims=True) + norm_eps)
    normed = (x_float * inv_rms * gain).astype(jnp.bfloat16)
    fsdp_pos = lax.axis_index("fsdp")
    place = tuple(
        jnp.reshape(value, (1,)).astype(jnp.int32)
        for value in (fsdp_pos // (2 * ring), fsdp_pos // 2 % ring, fsdp_pos % 2)
    )
    from_top = jnp.reshape(sections - 1 - section_pos, (1,)).astype(jnp.int32)
    weight, grads = top_grads(place, layer_in, normed, gathered, head, segs, labels)

    pieces = tokens // piece
    din = jnp.zeros((tokens, width), jnp.bfloat16)
    acc = jnp.zeros((extra, width), jnp.float32)
    received = {}
    blank = jnp.zeros((piece, width), jnp.bfloat16)
    for step in range(pieces + lag * (sections - 1)):
        out, grads, din, acc = chain_step(
            step,
            from_top,
            received.pop(step - lag, blank),
            weight,
            layer_in,
            inv_rms,
            gain[None],
            grads,
            din,
            acc,
        )
        pairs = [
            (s, s - 1)
            for s in range(1, sections)
            if any(
                0 <= near - lag * (sections - 1 - s) < pieces
                for near in range(step - step % merged, step - step % merged + merged)
            )
        ]
        if pairs:
            received[step] = lax.ppermute(out, "section", pairs)

    weight_part, gain_total = scatter_sum(place, normed.T, grads, acc, proj.shape[1])
    return (din[None], weight_part[None], gain_total)


def solution(mesh):
    return jax.shard_map(
        per_device,
        mesh=mesh,
        in_specs=(
            P("section", "fsdp", None),
            P("section", None),
            P("section", "fsdp", None),
            P(),
            P("fsdp", None),
            P("fsdp", None),
        ),
        out_specs=(P("section", "fsdp", None), P("section", "fsdp", None), P("section", None)),
        check_vma=False,
    )
```
